512 devices in a mesh: tm: 16 (over x_hi, y, core), height: 32 (over x_lo, z).
Axes of the slice: x: 4 (x_hi: 2, x_lo: 2; x = x_hi * 2 + x_lo), y: 4, z: 16, core: 2. Of those that a mesh axis runs over, the one named last changes fastest.
Arguments:
- queries: bfloat16 [16, 32, 128, 1536], P('tm', 'height'), may hold values from -6 to 6
- grad_out: bfloat16 [16, 32, 128, 1536], P('tm', 'height'), may hold values from -192 to 192
- key_value: bfloat16 [16, 32, 2, 128, 1536], P('tm', 'height'), may hold values from -6 to 6
- query_logsum: float32 [16, 32, 12, 128], P('tm', 'height'), may hold values from 6.5 to 8.5
- query_delta: float32 [16, 32, 12, 128], P('tm', 'height'), may hold values from -640 to 640
- window: int32 [16, 32, 4], replicated, may hold values from 0 to 1
- text_inputs: bfloat16 [3, 128, 1536], P(None, 'height'), may hold values from -6 to 6
- text_grad_out: bfloat16 [128, 1536], P('height'), may hold values from -192 to 192
- text_logsum: float32 [12, 128], replicated, may hold values from 9.5 to 11.5
- text_delta: float32 [12, 128], replicated, may hold values from -640 to 640
- text_length: int32 [1], replicated, may hold values from 32 to 128
Outputs:
- grad_queries: bfloat16 [16, 32, 128, 1536], P('tm', 'height')
- grad_key_value: bfloat16 [16, 32, 2, 128, 1536], P('tm', 'height')
- text_grads: float32 [3, 128, 1536], P(None, 'height')
The draws below stay inside these ranges and needn't reach their ends.
Inputs may be any that keep to these rules, and one draw needn't show every extreme that they name: `window`: each entry is a reach in tiles; reaches past the grid's edge are clipped. Text slots at or past text_length[0] are padding.
All inputs are finite; a program needn't handle non-finite values.
Results may differ from the reference program's by a relative error of at most 0.0057.
Values may be sent and summed in bfloat16 or wider, within the bound.
No kernel may reach another device: no remote copies, remote signals or barrier semaphores. Data moves between devices by JAX's collectives and lax.ppermute only.
A program may use at most 128 MiB of HBM per device.

```python
import jax
import jax.numpy as jnp
from jax import lax

HEADS = 12
FEATURES = 1536
TILE = 128
TEXT = 128
TIME_TILES = 16
HEIGHT_TILES = 32


def with_ends(drawn, rng, smallest, top_value):
    longest = drawn.shape.index(max(drawn.shape))
    spots = []
    for shift in (0, 1):
        where = [jax.random.randint(jax.random.fold_in(rng, axis), (), 0, length) for axis, length in enumerate(drawn.shape)]
        where[longest] = (where[longest] + shift) % drawn.shape[longest]
        spots.append(tuple(where))
    return drawn.at[spots[0]].set(smallest).at[spots[1]].set(top_value)


def block_scale(rng, shape, shards, least, high):
    factor_of = 1.0
    for axis_at, blocks in shards:
        heights = jax.random.uniform(jax.random.fold_in(jax.random.fold_in(rng, 6), axis_at), (blocks,), jnp.float32, least / len(shards), high / len(shards))
        factor_of = factor_of * jnp.repeat(jnp.exp(heights), shape[axis_at] // blocks).reshape((-1,) + (1,) * (len(shape) - 1 - axis_at))
    return factor_of


def centred(key, shape, deviation, bound, shards=(), held_as=jnp.bfloat16):
    result = jax.random.normal(key, shape, jnp.float32) * deviation
    if len(shards) > 0:
        result = block_scale(key, shape, shards, -0.22, 0.18) * result
    return jnp.clip(result, min=-bound, max=bound).astype(held_as)


def setup_inputs(seed: int = 0) -> dict:
    key_of = jax.random.split(jax.random.key(seed), 12)
    return {
        "queries": centred(key_of[0], (TIME_TILES, HEIGHT_TILES, TILE, FEATURES), 1.0, 6.0, ((0, 16), (1, 32))),
        "grad_out": centred(key_of[1], (TIME_TILES, HEIGHT_TILES, TILE, FEATURES), 32.0, 192.0, ((0, 16), (1, 32))),
        "key_value": centred(key_of[2], (TIME_TILES, HEIGHT_TILES, 2, TILE, FEATURES), 1.0, 6.0, ((0, 16), (1, 32))),
        "query_logsum": jnp.clip(6.5 + 2.0 * jax.random.uniform(key_of[3], (TIME_TILES, HEIGHT_TILES, HEADS, TILE), jnp.float32) ** block_scale(key_of[3], (TIME_TILES, HEIGHT_TILES, HEADS, TILE), ((0, 16), (1, 32)), -0.2, 0.2), 6.5, 8.5),
        "query_delta": centred(key_of[4], (TIME_TILES, HEIGHT_TILES, HEADS, TILE), 100.0, 640.0, ((0, 16), (1, 32)), jnp.float32),
        "window": with_ends(jax.random.randint(key_of[5], (TIME_TILES, HEIGHT_TILES, 4), 0, 2), jax.random.fold_in(key_of[5], 1), 0, 1).astype(jnp.int32),
        "text_inputs": centred(key_of[6], (3, TEXT, FEATURES), 1.0, 6.0, ((1, 32),)),
        "text_grad_out": centred(key_of[7], (TEXT, FEATURES), 32.0, 192.0, ((0, 32),)),
        "text_logsum": jnp.clip(jax.random.uniform(key_of[8], (HEADS, TEXT), jnp.float32, 9.5, 11.5), 9.5, 11.5),
        "text_delta": centred(key_of[9], (HEADS, TEXT), 100.0, 640.0, (), jnp.float32),
        "text_length": jax.random.randint(key_of[10], (1,), TEXT // 4, TEXT + 1).astype(jnp.int32),
    }


def block_grads(query_rows, cotangent, log_sums, row_delta, key_rows, value_rows, allowed, sources):
    head_count = log_sums.shape[0]
    row_count = query_rows.shape[0]
    head_size = query_rows.shape[1] // head_count
    score_scale = head_size ** -0.5
    per_source = row_count // sources
    query_heads = query_rows.astype(jnp.float32).reshape(row_count, head_count, head_size)
    cot_heads = cotangent.astype(jnp.float32).reshape(row_count, head_count, head_size)
    key_heads = key_rows.astype(jnp.float32).reshape(-1, head_count, head_size)
    value_heads = value_rows.astype(jnp.float32).reshape(-1, head_count, head_size)
    key_count = key_heads.shape[0]
    scores = jnp.einsum("qhd,khd->hqk", query_heads, key_heads) * score_scale
    weights = jnp.where(allowed[None], jnp.exp(scores - log_sums[:, :, None]), 0.0)
    d_weights = jnp.einsum("qhd,khd->hqk", cot_heads, value_heads)
    d_scores = weights * (d_weights - row_delta[:, :, None])
    weights_low, scores_low = lax.optimization_barrier((weights.astype(jnp.bfloat16), d_scores.astype(jnp.bfloat16)))
    weights_low = weights_low.astype(jnp.float32)
    scores_low = scores_low.astype(jnp.float32)
    query_grad = jnp.einsum("hqk,khd->qhd", scores_low, key_heads).reshape(row_count, -1) * score_scale
    score_source = scores_low.reshape(head_count, sources, per_source, key_count)
    weight_source = weights_low.reshape(head_count, sources, per_source, key_count)
    query_source = query_heads.reshape(sources, per_source, head_count, head_size)
    cot_source = cot_heads.reshape(sources, per_source, head_count, head_size)
    key_grad = jnp.einsum("hsqk,sqhd->skhd", score_source, query_source).reshape(sources, key_count, -1) * score_scale
    value_grad = jnp.einsum("hsqk,sqhd->skhd", weight_source, cot_source).reshape(sources, key_count, -1)
    return query_grad, key_grad, value_grad


def reference(queries, grad_out, key_value, query_logsum, query_delta, window, text_inputs, text_grad_out, text_logsum, text_delta, text_length):
    time_tiles, height_tiles, tile_rows, feat_width = queries.shape
    head_count = query_logsum.shape[2]
    text_count = text_inputs.shape[1]
    text_valid = jnp.arange(text_count) < text_length[0]
    padded = jnp.pad(key_value, ((1, 1), (1, 1), (0, 0), (0, 0), (0, 0)))
    offsets = jnp.arange(3, dtype=jnp.int32) - 1
    anchor = jnp.zeros((), jnp.int32)
    video_keys = 9 * tile_rows

    def tile_step(running, tile_index):
        key_grid, text_sum = running
        time_idx = (tile_index // height_tiles).astype(jnp.int32)
        height_idx = (tile_index % height_tiles).astype(jnp.int32)
        nearby = lax.dynamic_slice(padded, (time_idx, height_idx, anchor, anchor, anchor), (3, 3, 2, tile_rows, feat_width))
        extent = lax.dynamic_slice(window, (time_idx, height_idx, anchor), (1, 1, 4))[0, 0]
        along_time = (offsets >= -extent[0]) & (offsets <= extent[1]) & (time_idx + offsets >= 0) & (time_idx + offsets < time_tiles)
        along_height = (offsets >= -extent[2]) & (offsets <= extent[3]) & (height_idx + offsets >= 0) & (height_idx + offsets < height_tiles)
        tile_used = along_time[:, None] & along_height[None, :]
        key_used = jnp.concatenate([jnp.broadcast_to(tile_used[:, :, None], (3, 3, tile_rows)).reshape(-1), text_valid])
        key_rows = jnp.concatenate([nearby[:, :, 0].reshape(video_keys, feat_width), text_inputs[1]])
        value_rows = jnp.concatenate([nearby[:, :, 1].reshape(video_keys, feat_width), text_inputs[2]])
        own_queries = lax.dynamic_slice(queries, (time_idx, height_idx, anchor, anchor), (1, 1, tile_rows, feat_width))[0, 0]
        own_cot = lax.dynamic_slice(grad_out, (time_idx, height_idx, anchor, anchor), (1, 1, tile_rows, feat_width))[0, 0]
        own_logsum = lax.dynamic_slice(query_logsum, (time_idx, height_idx, anchor, anchor), (1, 1, head_count, tile_rows))[0, 0]
        own_delta = lax.dynamic_slice(query_delta, (time_idx, height_idx, anchor, anchor), (1, 1, head_count, tile_rows))[0, 0]
        query_grad, key_part, value_part = block_grads(own_queries, own_cot, own_logsum, own_delta, key_rows, value_rows, key_used[None, :], 1)
        contribution = jnp.stack([key_part[0, :video_keys].reshape(3, 3, tile_rows, feat_width), value_part[0, :video_keys].reshape(3, 3, tile_rows, feat_width)], axis=2)
        contribution = lax.optimization_barrier(contribution.astype(jnp.bfloat16)).astype(jnp.float32)
        text_query_grad, text_key_grad, text_value_grad = block_grads(text_inputs[0], text_grad_out, text_logsum, text_delta, nearby[1, 1, 0], nearby[1, 1, 1], text_valid[:, None], 1)
        contribution = contribution.at[1, 1].add(jnp.stack([text_key_grad[0], text_value_grad[0]]))
        previous = lax.dynamic_slice(key_grid, (time_idx, height_idx, anchor, anchor, anchor), (3, 3, 2, tile_rows, feat_width))
        key_grid = lax.dynamic_update_slice(key_grid, previous + contribution, (time_idx, height_idx, anchor, anchor, anchor))
        text_sum = text_sum + jnp.stack([text_query_grad, key_part[0, video_keys:], value_part[0, video_keys:]])
        return (key_grid, text_sum), query_grad.astype(jnp.bfloat16)

    grid_start = jnp.zeros((time_tiles + 2, height_tiles + 2, 2, tile_rows, feat_width), jnp.float32)
    text_start = jnp.zeros((3, text_count, feat_width), jnp.float32)
    (key_grid, text_sum), tile_grads = lax.scan(tile_step, (grid_start, text_start), jnp.arange(time_tiles * height_tiles, dtype=jnp.int32))
    grad_queries = tile_grads.reshape(time_tiles, height_tiles, tile_rows, feat_width)
    grad_key_value = key_grid[1:-1, 1:-1].astype(jnp.bfloat16)
    both_valid = text_valid[:, None] & text_valid[None, :]
    self_query, self_key, self_value = block_grads(text_inputs[0], text_grad_out, text_logsum, text_delta, text_inputs[1], text_inputs[2], both_valid, 1)
    text_grads = text_sum + jnp.stack([self_query, self_key[0], self_value[0]])
    return grad_queries, grad_key_value, text_grads
```

```python
import functools

import jax
import jax.numpy as jnp
from jax import lax
from jax.experimental import pallas as pl
from jax.experimental.pallas import tpu as pltpu
from jax.sharding import PartitionSpec as P

HEAD = 128
GROUP = 3
WIDE = HEAD * GROUP
STEPS = 4
STAT_ROWS = 16
FAR = 1e30
SCALE = HEAD**-0.5
LOG2E = 1.4426950408889634
SCORE = SCALE * LOG2E
VMEM_LIMIT = 40 * 1024 * 1024
F32 = jnp.float32
BF16 = jnp.bfloat16


def nt(a, b):
    return lax.dot_general(a, b, (((1,), (1,)), ((), ())), preferred_element_type=F32)


def nn(a, b):
    return lax.dot_general(a, b, (((1,), (0,)), ((), ())), preferred_element_type=F32)


def lanes(i):
    return slice(i * HEAD, (i + 1) * HEAD)


def column(row):
    return jnp.broadcast_to(row, (HEAD, row.shape[1])).T


def pair(a, b):
    return jnp.concatenate([a, b], axis=0)


def query_side(q, g, lse, delta, k, v, far):
    p = jnp.exp2(nt(q, k) * SCORE - far - lse)
    d = p * (nt(g, v) - delta)
    return nn(d.astype(BF16), k)


def key_side(k, v, q, g, lse, delta):
    p = jnp.exp2(nt(k, q) * SCORE - lse)
    d = p * (nt(v, g) - delta)
    return nn(d.astype(BF16), q), nn(p.astype(BF16), g)


def call(body, name, ins, outs, out_shape, scratch=(), flops=0, bytes_accessed=0, exps=0):
    return pl.pallas_call(
        body,
        name=name,
        grid=(STEPS,),
        in_specs=ins,
        out_specs=outs,
        out_shape=out_shape,
        scratch_shapes=list(scratch),
        compiler_params=pltpu.CompilerParams(vmem_limit_bytes=VMEM_LIMIT),
        cost_estimate=pl.CostEstimate(
            flops=flops, bytes_accessed=bytes_accessed, transcendentals=exps
        ),
    )


def rows_spec(rows):
    return pl.BlockSpec((rows, WIDE), lambda j: (0, j))


def two_spec(rows):
    return pl.BlockSpec((2, rows, WIDE), lambda j: (0, 0, j))


def stats_spec(rows):
    return pl.BlockSpec((1, rows, HEAD), lambda j: (j, 0, 0))


FAR_SPEC = pl.BlockSpec((32, HEAD), lambda j: (0, 0))
TEXT_SPEC = pl.BlockSpec((4, 1, HEAD, WIDE), lambda j: (0, j, 0, 0))


def pack_queries(q, g, lse, delta):
    tile = q.shape[0]

    def body(q_ref, g_ref, l_ref, d_ref, o_ref):
        o_ref[0:tile, :] = q_ref[...]
        o_ref[tile : 2 * tile, :] = g_ref[...]
        row = lax.broadcasted_iota(jnp.int32, (STAT_ROWS, HEAD), 0)
        for i in range(GROUP):
            slab = jnp.zeros((STAT_ROWS, HEAD), F32)
            at = 0
            for whole in (l_ref[0, i : i + 1, :] * LOG2E, d_ref[0, i : i + 1, :]):
                for _ in range(3):
                    part = whole.astype(BF16).astype(F32)
                    slab = jnp.where(row == at, part, slab)
                    whole = whole - part
                    at += 1
            o_ref[2 * tile :, lanes(i)] = slab.astype(BF16)

    rows = 2 * tile + STAT_ROWS
    return call(
        body,
        "pack_queries",
        [rows_spec(tile), rows_spec(tile), stats_spec(GROUP), stats_spec(GROUP)],
        rows_spec(rows),
        jax.ShapeDtypeStruct((rows, q.shape[1]), BF16),
        bytes_accessed=4 * tile * q.shape[1] * 2,
    )(q, g, lse, delta)


def read_stats(slab):
    slab = slab.astype(F32)
    lse = (slab[0:1] + slab[1:2]) + slab[2:3]
    delta = (slab[3:4] + slab[4:5]) + slab[5:6]
    return lse, delta


def text_terms(info, kv, pack, text, text_stats, far):
    tile = HEAD

    def body(info_ref, kv_ref, pack_ref, text_ref, stats_ref, far_ref, o_ref, sum_ref):
        step = pl.program_id(0)
        row = lax.broadcasted_iota(jnp.int32, (HEAD, HEAD), 0)
        valid = (row & 31) * 4 + (row >> 5) < info_ref[1]
        for i in range(GROUP):
            at = lanes(i)
            k, v = kv_ref[0:tile, at], kv_ref[tile : 2 * tile, at]
            q, g = pack_ref[0:tile, at], pack_ref[tile : 2 * tile, at]
            lse, delta = read_stats(pack_ref[2 * tile :, at])
            tq, tk, tv, tg = (text_ref[n, 0, :, at] for n in range(4))
            text_lse = stats_ref[0, i : i + 1, :]
            text_delta = stats_ref[0, GROUP + i : GROUP + i + 1, :]
            lse_rows, delta_rows = column(text_lse), column(text_delta)
            none = jnp.zeros((1, HEAD), F32)
            sum_ref[0] = query_side(tq, tg, lse_rows, delta_rows, k, v, none)
            sum_ref[1], sum_ref[2] = key_side(tk, tv, q, g, lse, delta)

            @pl.when(info_ref[0] == step * GROUP + i)
            def _():
                sum_ref[0] += query_side(tq, tg, lse_rows, delta_rows, tk, tv, far_ref[9:10, :])
                dk, dv = key_side(tk, tv, tq, tg, text_lse + far_ref[25:26, :], text_delta)
                sum_ref[1] += dk
                sum_ref[2] += dv

            for n in range(3):
                total = sum_ref[n] * SCALE if n < 2 else sum_ref[n]
                total = jnp.where(valid, total, 0.0).astype(BF16)
                for r in range(4):
                    o_ref[r, n, i] = total[r * 32 : (r + 1) * 32]

    return call(
        body,
        "text_terms",
        [
            pl.BlockSpec(memory_space=pltpu.SMEM),
            rows_spec(2 * tile),
            rows_spec(2 * tile + STAT_ROWS),
            TEXT_SPEC,
            stats_spec(2 * GROUP),
            FAR_SPEC,
        ],
        pl.BlockSpec((4, 3, GROUP, 32, HEAD), lambda j: (0, 0, j, 0, 0)),
        jax.ShapeDtypeStruct((4, 3, STEPS * GROUP, 32, HEAD), BF16),
        scratch=[pltpu.VMEM((3, HEAD, HEAD), F32)],
        flops=7 * 12 * 2 * 128**3,
        bytes_accessed=4_400_000,
        exps=2 * 12 * 128 * 128,
    )(info, kv, pack, text, text_stats, far)


def query_near(q, g, lse, delta, kv, text, from_below, from_above, from_before, from_after, far):
    tile = HEAD

    def body(q_ref, g_ref, l_ref, d_ref, kv_ref, text_ref, b_ref, a_ref, e_ref, f_ref, far_ref, o_ref):
        def key(ref, at):
            return ref[0:tile, at]

        def value(ref, at):
            return ref[tile : 2 * tile, at]

        def span(m, n):
            return jnp.concatenate([far_ref[m : m + 1, :], far_ref[n : n + 1, :]], axis=1)

        for i in range(GROUP):
            at = lanes(i)
            qh, gh = q_ref[:, at], g_ref[:, at]
            lse = column(l_ref[0, i : i + 1, :] * LOG2E)
            delta = column(d_ref[0, i : i + 1, :])
            lse = jnp.concatenate([lse, lse], axis=1)
            delta = jnp.concatenate([delta, delta], axis=1)
            total = query_side(
                qh, gh, lse, delta,
                pair(key(kv_ref, at), text_ref[1, 0, :, at]),
                pair(value(kv_ref, at), text_ref[2, 0, :, at]),
                span(4, 9),
            )
            for one, other, m, n in ((b_ref, a_ref, 3, 5), (e_ref, f_ref, 1, 7)):
                total += query_side(
                    qh, gh, lse, delta,
                    pair(key(one, at), key(other, at)),
                    pair(value(one, at), value(other, at)),
                    span(m, n),
                )
            o_ref[:, at] = total

    return call(
        body,
        "query_near",
        [rows_spec(tile)] * 2
        + [stats_spec(GROUP)] * 2
        + [rows_spec(2 * tile), TEXT_SPEC]
        + [rows_spec(2 * tile)] * 4
        + [FAR_SPEC],
        rows_spec(tile),
        jax.ShapeDtypeStruct(q.shape, F32),
        flops=18 * 12 * 2 * 128**3,
        bytes_accessed=7_000_000,
        exps=6 * 12 * 128 * 128,
    )(q, g, lse, delta, kv, text, from_below, from_above, from_before, from_after, far)


def query_far(q, g, lse, delta, before, after, far, near):
    tile = HEAD

    def body(q_ref, g_ref, l_ref, d_ref, e_ref, f_ref, far_ref, near_ref, o_ref):
        for i in range(GROUP):
            at = lanes(i)
            qh, gh = q_ref[:, at], g_ref[:, at]
            lse = column(l_ref[0, i : i + 1, :] * LOG2E)
            delta = column(d_ref[0, i : i + 1, :])
            lse = jnp.concatenate([lse, lse], axis=1)
            delta = jnp.concatenate([delta, delta], axis=1)
            total = near_ref[:, at]
            for ref, m, n in ((e_ref, 0, 2), (f_ref, 6, 8)):
                total += query_side(
                    qh, gh, lse, delta,
                    pair(ref[0, 0:tile, at], ref[1, 0:tile, at]),
                    pair(ref[0, tile : 2 * tile, at], ref[1, tile : 2 * tile, at]),
                    jnp.concatenate([far_ref[m : m + 1, :], far_ref[n : n + 1, :]], axis=1),
                )
            o_ref[:, at] = (total * SCALE).astype(BF16)

    return call(
        body,
        "query_far",
        [rows_spec(tile)] * 2
        + [stats_spec(GROUP)] * 2
        + [two_spec(2 * tile)] * 2
        + [FAR_SPEC, rows_spec(tile)],
        rows_spec(tile),
        jax.ShapeDtypeStruct(q.shape, BF16),
        flops=12 * 12 * 2 * 128**3,
        bytes_accessed=5_200_000,
        exps=4 * 12 * 128 * 128,
    )(q, g, lse, delta, before, after, far, near)


def key_near(kv, pack, text, text_stats, from_below, from_above, from_before, from_after, far):
    tile = HEAD

    def body(kv_ref, p_ref, text_ref, ts_ref, b_ref, a_ref, e_ref, f_ref, far_ref, o_ref):
        def part(ref, at, n):
            lse, delta = read_stats(ref[2 * tile :, at])
            lse = lse + far_ref[16 + n : 17 + n, :]
            return ref[0:tile, at], ref[tile : 2 * tile, at], lse, delta

        for i in range(GROUP):
            at = lanes(i)
            k, v = kv_ref[0:tile, at], kv_ref[tile : 2 * tile, at]
            text_part = (
                text_ref[0, 0, :, at],
                text_ref[3, 0, :, at],
                ts_ref[0, i : i + 1, :] + far_ref[25:26, :],
                ts_ref[0, GROUP + i : GROUP + i + 1, :],
            )
            dk = dv = 0.0
            for one, other in (
                (part(p_ref, at, 4), text_part),
                (part(b_ref, at, 3), part(a_ref, at, 5)),
                (part(e_ref, at, 1), part(f_ref, at, 7)),
            ):
                more_k, more_v = key_side(
                    k, v,
                    pair(one[0], other[0]),
                    pair(one[1], other[1]),
                    jnp.concatenate([one[2], other[2]], axis=1),
                    jnp.concatenate([one[3], other[3]], axis=1),
                )
                dk += more_k
                dv += more_v
            o_ref[0:tile, at] = dk
            o_ref[tile : 2 * tile, at] = dv

    pack_spec = rows_spec(2 * tile + STAT_ROWS)
    return call(
        body,
        "key_near",
        [rows_spec(2 * tile), pack_spec, TEXT_SPEC, stats_spec(2 * GROUP)]
        + [pack_spec] * 4
        + [FAR_SPEC],
        rows_spec(2 * tile),
        jax.ShapeDtypeStruct(kv.shape, F32),
        flops=24 * 12 * 2 * 128**3,
        bytes_accessed=7_800_000,
        exps=6 * 12 * 128 * 128,
    )(kv, pack, text, text_stats, from_below, from_above, from_before, from_after, far)


def key_far(kv, before, after, far, near):
    tile = HEAD

    def body(kv_ref, e_ref, f_ref, far_ref, near_ref, o_ref):
        for i in range(GROUP):
            at = lanes(i)
            k, v = kv_ref[0:tile, at], kv_ref[tile : 2 * tile, at]
            dk = near_ref[0:tile, at]
            dv = near_ref[tile : 2 * tile, at]
            for ref, m, n in ((e_ref, 16, 18), (f_ref, 22, 24)):
                lse0, delta0 = read_stats(ref[0, 2 * tile :, at])
                lse1, delta1 = read_stats(ref[1, 2 * tile :, at])
                more_k, more_v = key_side(
                    k, v,
                    pair(ref[0, 0:tile, at], ref[1, 0:tile, at]),
                    pair(ref[0, tile : 2 * tile, at], ref[1, tile : 2 * tile, at]),
                    jnp.concatenate(
                        [lse0 + far_ref[m : m + 1, :], lse1 + far_ref[n : n + 1, :]], axis=1
                    ),
                    jnp.concatenate([delta0, delta1], axis=1),
                )
                dk += more_k
                dv += more_v
            o_ref[0:tile, at] = (dk * SCALE).astype(BF16)
            o_ref[tile : 2 * tile, at] = dv.astype(BF16)

    return call(
        body,
        "key_far",
        [rows_spec(2 * tile)]
        + [two_spec(2 * tile + STAT_ROWS)] * 2
        + [FAR_SPEC, rows_spec(2 * tile)],
        rows_spec(2 * tile),
        jax.ShapeDtypeStruct(kv.shape, BF16),
        flops=16 * 12 * 2 * 128**3,
        bytes_accessed=6_500_000,
        exps=4 * 12 * 128 * 128,
    )(kv, before, after, far, near)


def from_neighbours(array, axis):
    count = lax.axis_size(axis)
    return (
        lax.ppermute(array, axis, [(i, i + 1) for i in range(count - 1)]),
        lax.ppermute(array, axis, [(i + 1, i) for i in range(count - 1)]),
    )


def exchange(array, axis):
    return lax.all_to_all(array, axis, 0, 0, tiled=True)


def gather_text(text_inputs, text_grad_out):
    t = lax.axis_index("tm")
    times, heights = lax.axis_size("tm"), lax.axis_size("height")
    share = text_grad_out.shape[0]
    text = jnp.concatenate([text_inputs, text_grad_out[None]], axis=0)
    piece = lax.dynamic_slice(text, (t // STEPS, 0, (t % STEPS) * WIDE), (1, share, WIDE))
    rows = exchange(jnp.broadcast_to(piece, (heights, share, WIDE)), "height")
    rows = rows.transpose(1, 0, 2).reshape(1, share * heights, WIDE)
    full = exchange(jnp.broadcast_to(rows, (times, share * heights, WIDE)), "tm")
    return full.reshape(4, STEPS, share * heights, WIDE)


def reduce_text(terms):
    times, heights = lax.axis_size("tm"), lax.axis_size("height")
    share, kinds, heads = terms.shape[:3]
    units = share * kinds * heads // times
    parts = exchange(terms.reshape(times, units, heights, HEAD), "tm")
    own = parts.astype(F32).sum(axis=0).transpose(1, 0, 2)
    own = exchange(own, "height").sum(axis=0)
    whole = exchange(jnp.broadcast_to(own[None], (times, units, HEAD)), "tm")
    return whole.reshape(share, kinds, heads * HEAD).transpose(1, 0, 2)


def penalties(window, text_length, t, h, times, heights, text_rows):
    step = jnp.arange(3) - 1
    at_t = t + step[:, None]
    at_h = h + step[None, :]
    inside = (at_t >= 0) & (at_t < times) & (at_h >= 0) & (at_h < heights)
    own = lax.dynamic_slice(window, (t, h, 0), (1, 1, 4))[0, 0]
    sees_t = (step >= -own[0]) & (step <= own[1])
    sees_h = (step >= -own[2]) & (step <= own[3])
    sees = sees_t[:, None] & sees_h[None, :] & inside
    around = lax.dynamic_slice(jnp.pad(window, ((1, 1), (1, 1), (0, 0))), (t, h, 0), (3, 3, 4))
    back_t, back_h = -step[:, None], -step[None, :]
    seen = (back_t >= -around[..., 0]) & (back_t <= around[..., 1])
    seen &= (back_h >= -around[..., 2]) & (back_h <= around[..., 3]) & inside
    place = jnp.arange(text_rows)
    share = text_rows // heights
    text = ((place % heights) * share + place // heights) < text_length[0]

    def block(tiles):
        rows = jnp.broadcast_to(tiles.reshape(9, 1), (9, text_rows))
        return jnp.concatenate([rows, text[None], jnp.zeros((6, text_rows), bool)])

    return jnp.where(jnp.concatenate([block(sees), block(seen)]), 0.0, FAR).astype(F32)


def on_device(
    queries,
    grad_out,
    key_value,
    query_logsum,
    query_delta,
    window,
    text_inputs,
    text_grad_out,
    text_logsum,
    text_delta,
    text_length,
):
    t, h = lax.axis_index("tm"), lax.axis_index("height")
    times, heights = lax.axis_size("tm"), lax.axis_size("height")
    tile, width = queries.shape[2:]
    heads = query_logsum.shape[2]
    text_rows = text_logsum.shape[1]

    q = queries.reshape(tile, width)
    g = grad_out.reshape(tile, width)
    kv = key_value.reshape(2 * tile, width)
    lse = query_logsum.reshape(STEPS, GROUP, tile)
    delta = query_delta.reshape(STEPS, GROUP, tile)

    kv_below, kv_above = from_neighbours(kv, "height")
    kv_before, kv_after = from_neighbours(kv, "tm")
    pack = pack_queries(q, g, lse, delta)
    pack_below, pack_above = from_neighbours(pack, "height")
    pack_before, pack_after = from_neighbours(pack, "tm")

    text = gather_text(text_inputs, text_grad_out)

    def by_group(stats):
        stats = stats.reshape(heads, heights, text_rows // heights).transpose(0, 2, 1)
        return stats.reshape(STEPS, GROUP, text_rows)

    text_stats = jnp.concatenate([by_group(text_logsum) * LOG2E, by_group(text_delta)], axis=1)
    far = penalties(window, text_length, t, h, times, heights, text_rows)
    info = jnp.stack([t * heights + h, text_length[0]]).astype(jnp.int32)

    terms = text_terms(info, kv, pack, text, text_stats, far)

    kv_far_before, kv_far_after = from_neighbours(jnp.stack([kv_below, kv_above]), "tm")
    pack_far_before, pack_far_after = from_neighbours(jnp.stack([pack_below, pack_above]), "tm")

    text_grads = reduce_text(terms)

    near_q = query_near(q, g, lse, delta, kv, text, kv_below, kv_above, kv_before, kv_after, far)
    near_k = key_near(
        kv, pack, text, text_stats, pack_below, pack_above, pack_before, pack_after, far
    )
    grad_q = query_far(q, g, lse, delta, kv_far_before, kv_far_after, far, near_q)
    grad_kv = key_far(kv, pack_far_before, pack_far_after, far, near_k)
    return (
        grad_q.reshape(1, 1, tile, width),
        grad_kv.reshape(1, 1, 2, tile, width),
        text_grads,
    )


def solution(mesh):
    placed = (
        P("tm", "height", None, None),
        P("tm", "height", None, None),
        P("tm", "height", None, None, None),
        P("tm", "height", None, None),
        P("tm", "height", None, None),
        P(),
        P(None, "height", None),
        P("height", None),
        P(),
        P(),
        P(),
    )
    return jax.shard_map(
        on_device,
        mesh=mesh,
        in_specs=placed,
        out_specs=(
            P("tm", "height", None, None),
            P("tm", "height", None, None, None),
            P(None, "height", None),
        ),
        check_vma=False,
    )
```

```python
import functools

import jax
import jax.numpy as jnp
from jax import lax
from jax.experimental import pallas as pl
from jax.experimental.pallas import tpu as pltpu
from jax.sharding import PartitionSpec as P

HEAD = 128
GROUP = 3
WIDE = HEAD * GROUP
STEPS = 4
STAT_ROWS = 16
FAR = 1e30
SCALE = HEAD**-0.5
LOG2E = 1.4426950408889634
SCORE = SCALE * LOG2E
VMEM_LIMIT = 16 * 1024 * 1024
F32 = jnp.float32
BF16 = jnp.bfloat16


def nt(a, b):
    return lax.dot_general(a, b, (((1,), (1,)), ((), ())), preferred_element_type=F32)


def nn(a, b):
    return lax.dot_general(a, b, (((1,), (0,)), ((), ())), preferred_element_type=F32)


def lanes(i):
    return slice(i * HEAD, (i + 1) * HEAD)


def column(row):
    return jnp.broadcast_to(row, (HEAD, row.shape[1])).T


def pair(a, b):
    return jnp.concatenate([a, b], axis=0)


def wide(a, b):
    return jnp.concatenate([a, b], axis=1)


def query_sides(q, g, lse, delta, parts):
    scores = [(nt(q, k), nt(g, v)) for k, v, _ in parts]
    grads = []
    for (s, w), (_, _, far) in zip(scores, parts):
        at = [x[:, : s.shape[1]] for x in (lse, delta)]
        p = jnp.exp2(s * SCORE - far - at[0])
        grads.append((p * (w - at[1])).astype(BF16))
    return functools.reduce(jnp.add, [nn(d, k) for d, (k, _, _) in zip(grads, parts)])


def key_sides(k, v, parts):
    scores = [(nt(k, q), nt(v, g)) for q, g, _, _ in parts]
    grads = []
    for (s, w), (_, _, lse, delta) in zip(scores, parts):
        p = jnp.exp2(s * SCORE - lse)
        grads.append(((p * (w - delta)).astype(BF16), p.astype(BF16)))
    dk = functools.reduce(jnp.add, [nn(d, q) for (d, _), (q, _, _, _) in zip(grads, parts)])
    dv = functools.reduce(jnp.add, [nn(p, g) for (_, p), (_, g, _, _) in zip(grads, parts)])
    return dk, dv


def call(body, name, ins, outs, out_shape, scratch=(), flops=0, bytes_accessed=0, exps=0):
    return pl.pallas_call(
        body,
        name=name,
        grid=(STEPS,),
        in_specs=ins,
        out_specs=outs,
        out_shape=out_shape,
        scratch_shapes=list(scratch),
        compiler_params=pltpu.CompilerParams(vmem_limit_bytes=VMEM_LIMIT),
        cost_estimate=pl.CostEstimate(
            flops=flops, bytes_accessed=bytes_accessed, transcendentals=exps
        ),
    )


def rows_spec(rows):
    return pl.BlockSpec((rows, WIDE), lambda j: (0, j))


def whole_spec(*shape):
    return pl.BlockSpec(shape, lambda j: (0,) * len(shape))


SCALARS = pl.BlockSpec(memory_space=pltpu.SMEM)
TEXT_SPEC = pl.BlockSpec((4, 1, HEAD, WIDE), lambda j: (0, j >> 1, 0, j & 1))
NEAR_TIMES = 8
TILE = HEAD
PACK_ROWS = 4 * TILE + STAT_ROWS
FAR_ROWS = 32
OWN, H1, H2, T1, T2, T1H1, T1H2, T2H1, T2H2, TEXT_PLACE = range(10)
QUERY_PLACES = 16


def pack_tile(info, window, kv, q, g, lse, delta):
    times, _, heights = window.shape
    text_rows = HEAD

    def body(info_ref, win_ref, kv_ref, q_ref, g_ref, l_ref, d_ref, o_ref, far_ref):
        step = pl.program_id(0)
        o_ref[0 : 2 * TILE, :] = kv_ref[...]
        o_ref[2 * TILE : 3 * TILE, :] = q_ref[...]
        o_ref[3 * TILE : 4 * TILE, :] = g_ref[...]
        row = lax.broadcasted_iota(jnp.int32, (STAT_ROWS, HEAD), 0)
        for i in range(GROUP):
            slab = jnp.zeros((STAT_ROWS, HEAD), F32)
            at = 0
            which = pl.ds(step * GROUP + i, 1)
            for rest in (l_ref[0, 0, which, :] * LOG2E, d_ref[0, 0, which, :]):
                for _ in range(3):
                    part = rest.astype(BF16).astype(F32)
                    slab = jnp.where(row == at, part, slab)
                    rest = rest - part
                    at += 1
            o_ref[4 * TILE :, lanes(i)] = slab.astype(BF16)

        @pl.when(step == 0)
        def _():
            t, h = info_ref[0], info_ref[1]
            a1, b1 = 1 - 2 * (t & 1), 1 - 2 * (h & 1)

            def sees(at_t, at_h, a, b):
                reach = [win_ref[at_t, n, at_h] for n in range(4)]
                return (a >= -reach[0]) & (a <= reach[1]) & (b >= -reach[2]) & (b <= reach[3])

            far_ref[...] = jnp.full((FAR_ROWS, HEAD), FAR, F32)
            places = ((0, 0), (0, b1), (0, -b1), (a1, 0), (-a1, 0))
            places += ((a1, b1), (a1, -b1), (-a1, b1), (-a1, -b1))
            for n, (a, b) in enumerate(places):
                at_t, at_h = t + a, h + b
                inside = (at_t >= 0) & (at_t < times) & (at_h >= 0) & (at_h < heights)
                at_t = jnp.clip(at_t, 0, times - 1)
                at_h = jnp.clip(at_h, 0, heights - 1)
                key = jnp.where(inside & sees(t, h, a, b), 0.0, FAR)
                query = jnp.where(inside & sees(at_t, at_h, -a, -b), 0.0, FAR)
                far_ref[n : n + 1, :] = jnp.full((1, HEAD), key, F32)
                far_ref[QUERY_PLACES + n : QUERY_PLACES + n + 1, :] = jnp.full((1, HEAD), query, F32)
            slot = lax.broadcasted_iota(jnp.int32, (1, text_rows), 1)
            text = jnp.where(slot < info_ref[2], 0.0, FAR)
            far_ref[TEXT_PLACE : TEXT_PLACE + 1, :] = text
            far_ref[QUERY_PLACES + TEXT_PLACE : QUERY_PLACES + TEXT_PLACE + 1, :] = text

    heads = lse.shape[2]
    return call(
        body,
        "pack_tile",
        [SCALARS, SCALARS, rows_spec(2 * TILE), rows_spec(TILE), rows_spec(TILE)]
        + [whole_spec(1, 1, heads, TILE)] * 2,
        [rows_spec(PACK_ROWS), whole_spec(FAR_ROWS, HEAD)],
        [
            jax.ShapeDtypeStruct((PACK_ROWS, q.shape[1]), BF16),
            jax.ShapeDtypeStruct((FAR_ROWS, HEAD), F32),
        ],
        bytes_accessed=8 * TILE * q.shape[1] * 2,
    )(info, window, kv, q, g, lse, delta)


def joined(arrays, *earlier):
    count = len(arrays)

    def body(*refs):
        o_ref = refs[-1]
        for n in range(count):
            o_ref[n] = refs[n][...]

    rows, width = arrays[0].shape
    return call(
        body,
        "joined",
        [rows_spec(rows)] * count + [pl.BlockSpec(memory_space=pl.ANY)] * len(earlier),
        pl.BlockSpec((count, rows, WIDE), lambda j: (0, 0, j)),
        jax.ShapeDtypeStruct((count, rows, width), BF16),
        bytes_accessed=4 * count * rows * width,
    )(*arrays, *earlier)


def keys_of(ref, at):
    return ref[0:TILE, at], ref[TILE : 2 * TILE, at]


def queries_of(ref, at):
    return ref[2 * TILE : 3 * TILE, at], ref[3 * TILE : 4 * TILE, at]


def stats_of(ref, at):
    slab = ref[4 * TILE :, at].astype(F32)
    lse = (slab[0:1] + slab[1:2]) + slab[2:3]
    delta = (slab[3:4] + slab[4:5]) + slab[5:6]
    return lse, delta


def far_of(far_ref, place, queries=False):
    row = place + (QUERY_PLACES if queries else 0)
    return far_ref[row : row + 1, :]


def key_pair(one, other):
    return pair(one[0], other[0]), pair(one[1], other[1]), wide(one[2], other[2])


def query_pair(one, other):
    return (
        pair(one[0], other[0]),
        pair(one[1], other[1]),
        wide(one[2], other[2]),
        wide(one[3], other[3]),
    )


def text_terms(info, pack, text, text_lse, text_delta, far):
    def body(info_ref, pack_ref, text_ref, tl_ref, td_ref, far_ref, o_ref, sum_ref):
        step = pl.program_id(0)
        linear = info_ref[3]
        row = lax.broadcasted_iota(jnp.int32, (HEAD, HEAD), 0)
        valid = row < info_ref[2]
        none = jnp.zeros((1, HEAD), F32)
        work = []
        for i in range(GROUP):
            at = lanes(i)
            which = pl.ds(step * GROUP + i, 1)
            tq, tk, tv, tg = (text_ref[n, 0, :, at] for n in range(4))
            lse, delta = tl_ref[which, :] * LOG2E, td_ref[which, :]
            work.append((tq, tk, tv, tg, lse, delta, column(lse), column(delta)))
        for i in range(GROUP):
            at = lanes(i)
            tq, tk, tv, tg, _, _, lse_rows, delta_rows = work[i]
            sum_ref[i, 0] = query_sides(
                tq, tg, lse_rows, delta_rows, [(*keys_of(pack_ref, at), none)]
            )
            sum_ref[i, 1], sum_ref[i, 2] = key_sides(
                tk, tv, [(*queries_of(pack_ref, at), *stats_of(pack_ref, at))]
            )
        for i in range(GROUP):
            tq, tk, tv, tg, lse, delta, lse_rows, delta_rows = work[i]

            @pl.when(linear == step * GROUP + i)
            def _():
                sum_ref[i, 0] += query_sides(
                    tq, tg, lse_rows, delta_rows, [(tk, tv, far_of(far_ref, TEXT_PLACE))]
                )
                masked = lse + far_of(far_ref, TEXT_PLACE, True)
                dk, dv = key_sides(tk, tv, [(tq, tg, masked, delta)])
                sum_ref[i, 1] += dk
                sum_ref[i, 2] += dv

        for i in range(GROUP):
            for n in range(3):
                total = sum_ref[i, n]
                total = total * SCALE if n < 2 else total
                sum_ref[i, n] = jnp.where(valid, total, 0.0)
                for r in range(4):
                    o_ref[r, n, i] = sum_ref[i, n, pl.ds(r, 32, stride=4), :].astype(BF16)

    heads = text_lse.shape[0]
    return call(
        body,
        "text_terms",
        [SCALARS, rows_spec(PACK_ROWS), TEXT_SPEC]
        + [whole_spec(heads, HEAD)] * 2
        + [whole_spec(FAR_ROWS, HEAD)],
        pl.BlockSpec((4, 3, GROUP, 32, HEAD), lambda j: (0, 0, j, 0, 0)),
        jax.ShapeDtypeStruct((4, 3, STEPS * GROUP, 32, HEAD), BF16),
        scratch=[pltpu.VMEM((GROUP, 3, HEAD, HEAD), F32)],
        flops=7 * 12 * 2 * 128**3,
        bytes_accessed=4_400_000,
        exps=2 * 12 * 128 * 128,
    )(info, pack, text, text_lse, text_delta, far)


def near_grads(pack, text, text_lse, text_delta, places, far):
    def body(p_ref, text_ref, tl_ref, td_ref, h1_ref, h2_ref, t1_ref, t2_ref, far_ref, o_ref):
        step = pl.program_id(0)
        for i in range(GROUP):
            at = lanes(i)
            which = pl.ds(step * GROUP + i, 1)
            q, g = queries_of(p_ref, at)
            k, v = keys_of(p_ref, at)
            lse, delta = stats_of(p_ref, at)
            lse_rows, delta_rows = column(lse), column(delta)

            def key(ref, place):
                return (*keys_of(ref, at), far_of(far_ref, place))

            def query(ref, place):
                more, d = stats_of(ref, at)
                return (*queries_of(ref, at), more + far_of(far_ref, place, True), d)

            text_key = (text_ref[1, 0, :, at], text_ref[2, 0, :, at], far_of(far_ref, TEXT_PLACE))
            text_query = (
                text_ref[0, 0, :, at],
                text_ref[3, 0, :, at],
                tl_ref[which, :] * LOG2E + far_of(far_ref, TEXT_PLACE, True),
                td_ref[which, :],
            )
            o_ref[0:TILE, at] = query_sides(
                q, g, wide(lse_rows, lse_rows), wide(delta_rows, delta_rows),
                [
                    key_pair(key(p_ref, OWN), text_key),
                    key_pair(key(h1_ref, H1), key(h2_ref, H2)),
                    key_pair(key(t1_ref, T1), key(t2_ref, T2)),
                ],
            )
            o_ref[TILE : 2 * TILE, at], o_ref[2 * TILE : 3 * TILE, at] = key_sides(
                k, v,
                [
                    query_pair(query(p_ref, OWN), text_query),
                    query_pair(query(h1_ref, H1), query(h2_ref, H2)),
                    query_pair(query(t1_ref, T1), query(t2_ref, T2)),
                ],
            )

    heads = text_lse.shape[0]
    return call(
        body,
        "near_grads",
        [rows_spec(PACK_ROWS), TEXT_SPEC]
        + [whole_spec(heads, HEAD)] * 2
        + [rows_spec(PACK_ROWS)] * 4
        + [whole_spec(FAR_ROWS, HEAD)],
        rows_spec(3 * TILE),
        jax.ShapeDtypeStruct((3 * TILE, pack.shape[1]), F32),
        flops=42 * 12 * 2 * 128**3,
        bytes_accessed=12_000_000,
        exps=12 * 12 * 128 * 128,
    )(pack, text, text_lse, text_delta, *places, far)


def far_grads(pack, corner1, corner2, far, near):
    def body(p_ref, c1_ref, c2_ref, far_ref, near_ref, q_ref, kv_ref):
        for i in range(GROUP):
            at = lanes(i)
            q, g = queries_of(p_ref, at)
            k, v = keys_of(p_ref, at)
            lse, delta = stats_of(p_ref, at)
            lse_rows, delta_rows = column(lse), column(delta)

            def key(ref, place):
                return (*keys_of(ref, at), far_of(far_ref, place))

            def query(ref, place):
                more, d = stats_of(ref, at)
                return (*queries_of(ref, at), more + far_of(far_ref, place, True), d)

            refs = (
                ((c1_ref.at[0], T1H1), (c1_ref.at[1], T1H2)),
                ((c2_ref.at[0], T2H1), (c2_ref.at[1], T2H2)),
            )
            dq = near_ref[0:TILE, at] + query_sides(
                q, g, wide(lse_rows, lse_rows), wide(delta_rows, delta_rows),
                [key_pair(key(*one), key(*other)) for one, other in refs],
            )
            dk, dv = key_sides(
                k, v, [query_pair(query(*one), query(*other)) for one, other in refs]
            )
            q_ref[:, at] = (dq * SCALE).astype(BF16)
            kv_ref[0:TILE, at] = ((near_ref[TILE : 2 * TILE, at] + dk) * SCALE).astype(BF16)
            kv_ref[TILE : 2 * TILE, at] = (near_ref[2 * TILE : 3 * TILE, at] + dv).astype(BF16)

    two = pl.BlockSpec((2, PACK_ROWS, WIDE), lambda j: (0, 0, j))
    width = pack.shape[1]
    return call(
        body,
        "far_grads",
        [rows_spec(PACK_ROWS), two, two, whole_spec(FAR_ROWS, HEAD), rows_spec(3 * TILE)],
        [rows_spec(TILE), rows_spec(2 * TILE)],
        [
            jax.ShapeDtypeStruct((TILE, width), BF16),
            jax.ShapeDtypeStruct((2 * TILE, width), BF16),
        ],
        flops=28 * 12 * 2 * 128**3,
        bytes_accessed=12_000_000,
        exps=8 * 12 * 128 * 128,
    )(pack, corner1, corner2, far, near)


def swapped(array, axis):
    count = lax.axis_size(axis)
    both = []
    for first in (0, 1):
        pairs = []
        for i in range(first, count - 1, 2):
            pairs += [(i, i + 1), (i + 1, i)]
        both.append(lax.ppermute(array, axis, pairs))
    return both


def exchange(array, axis, group=None):
    count = lax.axis_size(axis)
    runs = None
    if group is not None:
        runs = [list(range(i, i + group)) for i in range(0, count, group)]
    return lax.all_to_all(array, axis, 0, 0, axis_index_groups=runs, tiled=True)


def text_piece(text_inputs, text_grad_out):
    place = lax.axis_index("tm") & (NEAR_TIMES - 1)
    heights = lax.axis_size("height")
    share, width = text_grad_out.shape
    text = jnp.concatenate([text_inputs, text_grad_out[None]], axis=0)
    start = (place >> 1, 0, (place & 1) * (width // 2))
    piece = lax.dynamic_slice(text, start, (1, share, width // 2))
    rows = exchange(jnp.broadcast_to(piece, (heights, share, width // 2)), "height")
    return rows.reshape(1, share * heights, width // 2)


def text_whole(rows):
    full = exchange(jnp.broadcast_to(rows, (NEAR_TIMES, *rows.shape[1:])), "tm", NEAR_TIMES)
    return full.reshape(4, 2, *rows.shape[1:])


def reduce_times(terms):
    heights, lane = terms.shape[3:]
    return exchange(terms.reshape(NEAR_TIMES, -1, heights, lane), "tm", NEAR_TIMES)


def summed(parts, earlier):
    shape = parts.shape[1:]

    def body(p_ref, _, o_ref):
        for u in range(shape[0]):
            total = p_ref[0, u].astype(F32)
            for n in range(1, parts.shape[0]):
                total += p_ref[n, u].astype(F32)
            o_ref[u] = total

    return pl.pallas_call(
        body,
        name="summed",
        in_specs=[pl.BlockSpec(memory_space=pltpu.VMEM), pl.BlockSpec(memory_space=pl.ANY)],
        out_specs=pl.BlockSpec(memory_space=pltpu.VMEM),
        out_shape=jax.ShapeDtypeStruct(shape, F32),
        compiler_params=pltpu.CompilerParams(vmem_limit_bytes=VMEM_LIMIT),
        cost_estimate=pl.CostEstimate(flops=0, bytes_accessed=1_500_000, transcendentals=0),
    )(parts, earlier)


def reduce_heights(own, shape):
    times = lax.axis_size("tm")
    share, kinds, heads = shape
    own = exchange(own.transpose(1, 0, 2), "height").sum(axis=0)
    whole = exchange(jnp.broadcast_to(own[None], (times, *own.shape)), "tm")
    whole = whole.reshape(times // NEAR_TIMES, -1, own.shape[-1]).sum(axis=0)
    return whole.reshape(share, kinds, heads * own.shape[-1]).transpose(1, 0, 2)


def on_device(
    queries,
    grad_out,
    key_value,
    query_logsum,
    query_delta,
    window,
    text_inputs,
    text_grad_out,
    text_logsum,
    text_delta,
    text_length,
):
    t, h = lax.axis_index("tm"), lax.axis_index("height")
    heights = lax.axis_size("height")
    tile, width = queries.shape[2:]

    q = queries.reshape(tile, width)
    g = grad_out.reshape(tile, width)
    kv = key_value.reshape(2 * tile, width)
    info = jnp.stack([t, h, text_length[0], t * heights + h]).astype(jnp.int32)

    piece = text_piece(text_inputs, text_grad_out)
    pack, far = pack_tile(
        info, window.transpose(0, 2, 1), kv, q, g, query_logsum, query_delta
    )
    t1, t2 = swapped(pack, "tm")
    h1, h2 = swapped(joined([pack], t1)[0], "height")
    text = text_whole(piece)

    terms = text_terms(info, pack, text, text_logsum, text_delta, far)
    parts = reduce_times(terms)
    corner1, corner2 = swapped(joined([h1, h2], t1, t2, parts), "tm")
    near = near_grads(pack, text, text_logsum, text_delta, (h1, h2, t1, t2), far)
    text_grads = reduce_heights(summed(parts, near), terms.shape[:3])
    grad_q, grad_kv = far_grads(pack, corner1, corner2, far, near)
    return (
        grad_q.reshape(1, 1, tile, width),
        grad_kv.reshape(1, 1, 2, tile, width),
        text_grads,
    )


def solution(mesh):
    placed = (
        P("tm", "height", None, None),
        P("tm", "height", None, None),
        P("tm", "height", None, None, None),
        P("tm", "height", None, None),
        P("tm", "height", None, None),
        P(),
        P(None, "height", None),
        P("height", None),
        P(),
        P(),
        P(),
    )
    return jax.shard_map(
        on_device,
        mesh=mesh,
        in_specs=placed,
        out_specs=(
            P("tm", "height", None, None),
            P("tm", "height", None, None, None),
            P(None, "height", None),
        ),
        check_vma=False,
    )
```

```python
import functools

import jax
import jax.numpy as jnp
from jax import lax
from jax.experimental import pallas as pl
from jax.experimental.pallas import tpu as pltpu
from jax.sharding import PartitionSpec as P

HEAD = 128
GROUP = 3
WIDE = HEAD * GROUP
STEPS = 4
STAT_ROWS = 16
FAR = 1e30
SCALE = HEAD**-0.5
LOG2E = 1.4426950408889634
SCORE = SCALE * LOG2E
VMEM_LIMIT = 16 * 1024 * 1024
F32 = jnp.float32
BF16 = jnp.bfloat16


def nt(a, b):
    return lax.dot_general(a, b, (((1,), (1,)), ((), ())), preferred_element_type=F32)


def nn(a, b):
    return lax.dot_general(a, b, (((1,), (0,)), ((), ())), preferred_element_type=F32)


def lanes(i):
    return slice(i * HEAD, (i + 1) * HEAD)


def column(row):
    return jnp.broadcast_to(row, (HEAD, row.shape[1])).T


def pair(a, b):
    return jnp.concatenate([a, b], axis=0)


def wide(a, b):
    return jnp.concatenate([a, b], axis=1)


def query_scores(q, g, parts):
    return [(nt(q, k), nt(g, v)) for k, v, _ in parts]


def query_sum(scores, lse, delta, parts):
    grads = []
    for (s, w), (_, _, far) in zip(scores, parts):
        at = [x if x.shape[1] == s.shape[1] else wide(x, x) for x in (lse, delta)]
        p = jnp.exp2(s * SCORE - far - at[0])
        grads.append((p * (w - at[1])).astype(BF16))
    return functools.reduce(jnp.add, [nn(d, k) for d, (k, _, _) in zip(grads, parts)])


def key_scores(k, v, parts):
    return [(nt(k, q), nt(v, g)) for q, g, _, _ in parts]


def key_sums(scores, parts):
    grads = []
    for (s, w), (_, _, lse, delta) in zip(scores, parts):
        p = jnp.exp2(s * SCORE - lse)
        grads.append(((p * (w - delta)).astype(BF16), p.astype(BF16)))
    dk = functools.reduce(jnp.add, [nn(d, q) for (d, _), (q, _, _, _) in zip(grads, parts)])
    dv = functools.reduce(jnp.add, [nn(p, g) for (_, p), (_, g, _, _) in zip(grads, parts)])
    return dk, dv


def staggered(start, finish):
    held = start(0)
    for i in range(GROUP):
        later = start(i + 1) if i + 1 < GROUP else None
        finish(i, held)
        held = later


def call(body, name, ins, outs, out_shape, scratch=(), flops=0, bytes_accessed=0, exps=0):
    return pl.pallas_call(
        body,
        name=name,
        grid=(STEPS,),
        in_specs=ins,
        out_specs=outs,
        out_shape=out_shape,
        scratch_shapes=list(scratch),
        compiler_params=pltpu.CompilerParams(vmem_limit_bytes=VMEM_LIMIT),
        cost_estimate=pl.CostEstimate(
            flops=flops, bytes_accessed=bytes_accessed, transcendentals=exps
        ),
    )


def rows_spec(rows):
    return pl.BlockSpec((rows, WIDE), lambda j: (0, j))


def whole_spec(*shape):
    return pl.BlockSpec(shape, lambda j: (0,) * len(shape))


SCALARS = pl.BlockSpec(memory_space=pltpu.SMEM)
ANYWHERE = pl.BlockSpec(memory_space=pl.ANY)
TEXT_SPEC = pl.BlockSpec((4, 1, HEAD, WIDE), lambda j: (0, j >> 1, 0, j & 1))
NEAR_TIMES = 8
TILE = HEAD
PACK_ROWS = 4 * TILE + STAT_ROWS
FAR_ROWS = 32
OWN, H1, H2, T1, T2, T1H1, T1H2, T2H1, T2H2, TEXT_PLACE = range(10)
QUERY_PLACES = 16


def pack_tile(info, window, kv, q, g, lse, delta, earlier):
    times, _, heights = window.shape
    text_rows = HEAD

    heads = lse.shape[2]

    def body(info_ref, win_ref, kv_ref, q_ref, g_ref, l_ref, d_ref, _, o_ref, far_ref, slab_ref, sems):
        moves = [
            pltpu.make_async_copy(kv_ref, o_ref.at[0 : 2 * TILE], sems.at[0]),
            pltpu.make_async_copy(q_ref, o_ref.at[2 * TILE : 3 * TILE], sems.at[1]),
            pltpu.make_async_copy(g_ref, o_ref.at[3 * TILE : 4 * TILE], sems.at[2]),
        ]
        for move in moves:
            move.start()
        row = lax.broadcasted_iota(jnp.int32, (STAT_ROWS, HEAD), 0)
        for i in range(heads):
            slab = jnp.zeros((STAT_ROWS, HEAD), F32)
            at = 0
            for rest in (l_ref[0, 0, i : i + 1, :] * LOG2E, d_ref[0, 0, i : i + 1, :]):
                for _ in range(3):
                    part = rest.astype(BF16).astype(F32)
                    slab = jnp.where(row == at, part, slab)
                    rest = rest - part
                    at += 1
            slab_ref[:, lanes(i)] = slab.astype(BF16)
        last = pltpu.make_async_copy(slab_ref, o_ref.at[4 * TILE : PACK_ROWS], sems.at[3])
        last.start()

        t, h = info_ref[0], info_ref[1]
        a1, b1 = 1 - 2 * (t & 1), 1 - 2 * (h & 1)

        def sees(at_t, at_h, a, b):
            reach = [win_ref[at_t, n, at_h] for n in range(4)]
            return (a >= -reach[0]) & (a <= reach[1]) & (b >= -reach[2]) & (b <= reach[3])

        far_ref[...] = jnp.full((FAR_ROWS, HEAD), FAR, F32)
        places = ((0, 0), (0, b1), (0, -b1), (a1, 0), (-a1, 0))
        places += ((a1, b1), (a1, -b1), (-a1, b1), (-a1, -b1))
        for n, (a, b) in enumerate(places):
            at_t, at_h = t + a, h + b
            inside = (at_t >= 0) & (at_t < times) & (at_h >= 0) & (at_h < heights)
            at_t = jnp.clip(at_t, 0, times - 1)
            at_h = jnp.clip(at_h, 0, heights - 1)
            key = jnp.where(inside & sees(t, h, a, b), 0.0, FAR)
            query = jnp.where(inside & sees(at_t, at_h, -a, -b), 0.0, FAR)
            far_ref[n : n + 1, :] = jnp.full((1, HEAD), key, F32)
            far_ref[QUERY_PLACES + n : QUERY_PLACES + n + 1, :] = jnp.full((1, HEAD), query, F32)
        slot = lax.broadcasted_iota(jnp.int32, (1, text_rows), 1)
        text = jnp.where(slot < info_ref[2], 0.0, FAR)
        far_ref[TEXT_PLACE : TEXT_PLACE + 1, :] = text
        far_ref[QUERY_PLACES + TEXT_PLACE : QUERY_PLACES + TEXT_PLACE + 1, :] = text

        for move in moves:
            move.wait()
        last.wait()

    vmem = pl.BlockSpec(memory_space=pltpu.VMEM)
    return pl.pallas_call(
        body,
        name="pack_tile",
        in_specs=[SCALARS, SCALARS, ANYWHERE, ANYWHERE, ANYWHERE, vmem, vmem, ANYWHERE],
        out_specs=[ANYWHERE, vmem],
        out_shape=[
            jax.ShapeDtypeStruct((PACK_ROWS, q.shape[1]), BF16),
            jax.ShapeDtypeStruct((FAR_ROWS, HEAD), F32),
        ],
        scratch_shapes=[
            pltpu.VMEM((STAT_ROWS, q.shape[1]), BF16),
            pltpu.SemaphoreType.DMA((4,)),
        ],
        compiler_params=pltpu.CompilerParams(vmem_limit_bytes=VMEM_LIMIT),
        cost_estimate=pl.CostEstimate(
            flops=0, bytes_accessed=8 * TILE * q.shape[1] * 2, transcendentals=0
        ),
    )(info, window, kv, q, g, lse, delta, earlier)


def joined(arrays, *earlier):
    count = len(arrays)

    def body(*refs):
        o_ref = refs[-1]
        for n in range(count):
            o_ref[n] = refs[n][...]

    rows, width = arrays[0].shape
    return call(
        body,
        "joined",
        [rows_spec(rows)] * count + [ANYWHERE] * len(earlier),
        pl.BlockSpec((count, rows, WIDE), lambda j: (0, 0, j)),
        jax.ShapeDtypeStruct((count, rows, width), BF16),
        bytes_accessed=4 * count * rows * width,
    )(*arrays, *earlier)


def keys_of(ref, at):
    return ref[0:TILE, at], ref[TILE : 2 * TILE, at]


def queries_of(ref, at):
    return ref[2 * TILE : 3 * TILE, at], ref[3 * TILE : 4 * TILE, at]


def stats_of(ref, at):
    slab = ref[4 * TILE :, at].astype(F32)
    lse = (slab[0:1] + slab[1:2]) + slab[2:3]
    delta = (slab[3:4] + slab[4:5]) + slab[5:6]
    return lse, delta


def far_of(far_ref, place, queries=False):
    row = place + (QUERY_PLACES if queries else 0)
    return far_ref[row : row + 1, :]


def key_pair(one, other):
    return pair(one[0], other[0]), pair(one[1], other[1]), wide(one[2], other[2])


def query_pair(one, other):
    return (
        pair(one[0], other[0]),
        pair(one[1], other[1]),
        wide(one[2], other[2]),
        wide(one[3], other[3]),
    )


def text_terms(info, pack, text, text_lse, text_delta, far):
    def body(info_ref, pack_ref, text_ref, tl_ref, td_ref, far_ref, o_ref, sum_ref):
        step = pl.program_id(0)
        linear = info_ref[3]
        row = lax.broadcasted_iota(jnp.int32, (HEAD, HEAD), 0)
        valid = row < info_ref[2]
        none = jnp.zeros((1, HEAD), F32)
        work = []
        for i in range(GROUP):
            at = lanes(i)
            which = pl.ds(step * GROUP + i, 1)
            tq, tk, tv, tg = (text_ref[n, 0, :, at] for n in range(4))
            lse, delta = tl_ref[which, :] * LOG2E, td_ref[which, :]
            work.append((tq, tk, tv, tg, lse, delta, column(lse), column(delta)))

        def start(i):
            at = lanes(i)
            tq, tk, tv, tg = work[i][:4]
            keys = [(*keys_of(pack_ref, at), none)]
            mine = [(*queries_of(pack_ref, at), *stats_of(pack_ref, at))]
            return query_scores(tq, tg, keys), keys, key_scores(tk, tv, mine), mine

        def finish(i, held):
            query, keys, key, mine = held
            sum_ref[i, 0] = query_sum(query, work[i][6], work[i][7], keys)
            sum_ref[i, 1], sum_ref[i, 2] = key_sums(key, mine)

        staggered(start, finish)
        for i in range(GROUP):
            tq, tk, tv, tg, lse, delta, lse_rows, delta_rows = work[i]

            @pl.when(linear == step * GROUP + i)
            def _():
                keys = [(tk, tv, far_of(far_ref, TEXT_PLACE))]
                sum_ref[i, 0] += query_sum(query_scores(tq, tg, keys), lse_rows, delta_rows, keys)
                mine = [(tq, tg, lse + far_of(far_ref, TEXT_PLACE, True), delta)]
                dk, dv = key_sums(key_scores(tk, tv, mine), mine)
                sum_ref[i, 1] += dk
                sum_ref[i, 2] += dv

        for i in range(GROUP):
            for n in range(3):
                total = sum_ref[i, n]
                total = total * SCALE if n < 2 else total
                sum_ref[i, n] = jnp.where(valid, total, 0.0)
                for r in range(4):
                    o_ref[r, n, i] = sum_ref[i, n, pl.ds(r, 32, stride=4), :].astype(BF16)

    heads = text_lse.shape[0]
    return call(
        body,
        "text_terms",
        [SCALARS, rows_spec(PACK_ROWS), TEXT_SPEC]
        + [whole_spec(heads, HEAD)] * 2
        + [whole_spec(FAR_ROWS, HEAD)],
        pl.BlockSpec((4, 3, GROUP, 32, HEAD), lambda j: (0, 0, j, 0, 0)),
        jax.ShapeDtypeStruct((4, 3, STEPS * GROUP, 32, HEAD), BF16),
        scratch=[pltpu.VMEM((GROUP, 3, HEAD, HEAD), F32)],
        flops=7 * 12 * 2 * 128**3,
        bytes_accessed=4_400_000,
        exps=2 * 12 * 128 * 128,
    )(info, pack, text, text_lse, text_delta, far)


def near_grads(pack, text, text_lse, text_delta, places, far):
    def body(p_ref, text_ref, tl_ref, td_ref, h1_ref, h2_ref, t1_ref, t2_ref, far_ref, o_ref):
        step = pl.program_id(0)

        def start(i):
            at = lanes(i)
            which = pl.ds(step * GROUP + i, 1)
            q, g = queries_of(p_ref, at)
            k, v = keys_of(p_ref, at)

            def key(ref, place):
                return (*keys_of(ref, at), far_of(far_ref, place))

            def query(ref, place):
                more, d = stats_of(ref, at)
                return (*queries_of(ref, at), more + far_of(far_ref, place, True), d)

            text_key = (text_ref[1, 0, :, at], text_ref[2, 0, :, at], far_of(far_ref, TEXT_PLACE))
            text_query = (
                text_ref[0, 0, :, at],
                text_ref[3, 0, :, at],
                tl_ref[which, :] * LOG2E + far_of(far_ref, TEXT_PLACE, True),
                td_ref[which, :],
            )
            keys = [
                key_pair(key(p_ref, OWN), text_key),
                key_pair(key(h1_ref, H1), key(h2_ref, H2)),
                key_pair(key(t1_ref, T1), key(t2_ref, T2)),
            ]
            mine = [
                query_pair(query(p_ref, OWN), text_query),
                query_pair(query(h1_ref, H1), query(h2_ref, H2)),
                query_pair(query(t1_ref, T1), query(t2_ref, T2)),
            ]
            return query_scores(q, g, keys), keys, key_scores(k, v, mine), mine

        def finish(i, held):
            at = lanes(i)
            query, keys, key, mine = held
            lse, delta = stats_of(p_ref, at)
            o_ref[0:TILE, at] = query_sum(query, column(lse), column(delta), keys)
            o_ref[TILE : 2 * TILE, at], o_ref[2 * TILE : 3 * TILE, at] = key_sums(key, mine)

        staggered(start, finish)

    heads = text_lse.shape[0]
    return call(
        body,
        "near_grads",
        [rows_spec(PACK_ROWS), TEXT_SPEC]
        + [whole_spec(heads, HEAD)] * 2
        + [rows_spec(PACK_ROWS)] * 4
        + [whole_spec(FAR_ROWS, HEAD)],
        rows_spec(3 * TILE),
        jax.ShapeDtypeStruct((3 * TILE, pack.shape[1]), F32),
        flops=42 * 12 * 2 * 128**3,
        bytes_accessed=12_000_000,
        exps=12 * 12 * 128 * 128,
    )(pack, text, text_lse, text_delta, *places, far)


def far_grads(pack, corner1, corner2, far, near):
    def body(p_ref, c1_ref, c2_ref, far_ref, near_ref, q_ref, kv_ref, done_ref):
        done_ref[...] = far_ref[0:8, :]
        refs = (
            ((c1_ref.at[0], T1H1), (c1_ref.at[1], T1H2)),
            ((c2_ref.at[0], T2H1), (c2_ref.at[1], T2H2)),
        )

        def start(i):
            at = lanes(i)
            q, g = queries_of(p_ref, at)
            k, v = keys_of(p_ref, at)

            def key(ref, place):
                return (*keys_of(ref, at), far_of(far_ref, place))

            def query(ref, place):
                more, d = stats_of(ref, at)
                return (*queries_of(ref, at), more + far_of(far_ref, place, True), d)

            keys = [key_pair(key(*one), key(*other)) for one, other in refs]
            mine = [query_pair(query(*one), query(*other)) for one, other in refs]
            return query_scores(q, g, keys), keys, key_scores(k, v, mine), mine

        def finish(i, held):
            at = lanes(i)
            query, keys, key, mine = held
            lse, delta = stats_of(p_ref, at)
            dq = near_ref[0:TILE, at] + query_sum(query, column(lse), column(delta), keys)
            dk, dv = key_sums(key, mine)
            q_ref[:, at] = (dq * SCALE).astype(BF16)
            kv_ref[0:TILE, at] = ((near_ref[TILE : 2 * TILE, at] + dk) * SCALE).astype(BF16)
            kv_ref[TILE : 2 * TILE, at] = (near_ref[2 * TILE : 3 * TILE, at] + dv).astype(BF16)

        staggered(start, finish)

    two = pl.BlockSpec((2, PACK_ROWS, WIDE), lambda j: (0, 0, j))
    width = pack.shape[1]
    return call(
        body,
        "far_grads",
        [rows_spec(PACK_ROWS), two, two, whole_spec(FAR_ROWS, HEAD), rows_spec(3 * TILE)],
        [rows_spec(TILE), rows_spec(2 * TILE), whole_spec(8, HEAD)],
        [
            jax.ShapeDtypeStruct((TILE, width), BF16),
            jax.ShapeDtypeStruct((2 * TILE, width), BF16),
            jax.ShapeDtypeStruct((8, HEAD), F32),
        ],
        flops=28 * 12 * 2 * 128**3,
        bytes_accessed=12_000_000,
        exps=8 * 12 * 128 * 128,
    )(pack, corner1, corner2, far, near)


def swapped(array, axis):
    count = lax.axis_size(axis)
    both = []
    for first in (0, 1):
        pairs = []
        for i in range(first, count - 1, 2):
            pairs += [(i, i + 1), (i + 1, i)]
        both.append(lax.ppermute(array, axis, pairs))
    return both


def exchange(array, axis, group=None):
    count = lax.axis_size(axis)
    runs = None
    if group is not None:
        runs = [list(range(i, i + group)) for i in range(0, count, group)]
    return lax.all_to_all(array, axis, 0, 0, axis_index_groups=runs, tiled=True)


def text_piece(text_inputs, text_grad_out):
    place = lax.axis_index("tm") & (NEAR_TIMES - 1)
    heights = lax.axis_size("height")
    share, width = text_grad_out.shape
    text = jnp.concatenate([text_inputs, text_grad_out[None]], axis=0)
    start = (place >> 1, 0, (place & 1) * (width // 2))
    piece = lax.dynamic_slice(text, start, (1, share, width // 2))
    rows = exchange(jnp.broadcast_to(piece, (heights, share, width // 2)), "height")
    return rows.reshape(1, share * heights, width // 2)


def text_whole(rows):
    full = exchange(jnp.broadcast_to(rows, (NEAR_TIMES, *rows.shape[1:])), "tm", NEAR_TIMES)
    return full.reshape(4, 2, *rows.shape[1:])


def reduce_times(terms):
    heights, lane = terms.shape[3:]
    return exchange(terms.reshape(NEAR_TIMES, -1, heights, lane), "tm", NEAR_TIMES)


def small(body, name, out_shape, array, earlier):
    return pl.pallas_call(
        body,
        name=name,
        in_specs=[pl.BlockSpec(memory_space=pltpu.VMEM), ANYWHERE],
        out_specs=pl.BlockSpec(memory_space=pltpu.VMEM),
        out_shape=out_shape,
        compiler_params=pltpu.CompilerParams(vmem_limit_bytes=VMEM_LIMIT),
        cost_estimate=pl.CostEstimate(flops=0, bytes_accessed=1_500_000, transcendentals=0),
    )(array, earlier)


def summed(parts, earlier):
    shape = parts.shape[1:]

    def body(p_ref, _, o_ref):
        for u in range(shape[0]):
            total = p_ref[0, u].astype(F32)
            for n in range(1, parts.shape[0]):
                total += p_ref[n, u].astype(F32)
            o_ref[u] = total.astype(BF16)

    return small(body, "summed", jax.ShapeDtypeStruct(shape, BF16), parts, earlier)


def summed_heights(parts, copies, earlier):
    count, units, lane = parts.shape

    def body(p_ref, _, o_ref):
        total = p_ref[0].astype(F32)
        for n in range(1, count):
            total += p_ref[n].astype(F32)
        for n in range(copies):
            o_ref[n] = total

    shape = jax.ShapeDtypeStruct((copies, units, lane), F32)
    return small(body, "summed_heights", shape, parts, earlier)


def placed_rows(parts, shape, earlier):
    share, kinds, heads = shape
    members, units, lane = parts.shape
    places = units * NEAR_TIMES // share

    def body(p_ref, _, o_ref):
        for place in range(NEAR_TIMES):
            total = p_ref[place]
            for run in range(1, members // NEAR_TIMES):
                total += p_ref[run * NEAR_TIMES + place]
            for u in range(units):
                at = place * units + u
                row, unit = at // places, at % places
                o_ref[unit // heads, row : row + 1, lanes(unit % heads)] = total[u : u + 1]

    out = jax.ShapeDtypeStruct((kinds, share, heads * lane), F32)
    return small(body, "placed_rows", out, parts, earlier)


def on_device(
    queries,
    grad_out,
    key_value,
    query_logsum,
    query_delta,
    window,
    text_inputs,
    text_grad_out,
    text_logsum,
    text_delta,
    text_length,
):
    t, h = lax.axis_index("tm"), lax.axis_index("height")
    heights = lax.axis_size("height")
    tile, width = queries.shape[2:]

    q = queries.reshape(tile, width)
    g = grad_out.reshape(tile, width)
    kv = key_value.reshape(2 * tile, width)
    info = jnp.stack([t, h, text_length[0], t * heights + h]).astype(jnp.int32)

    piece = text_piece(text_inputs, text_grad_out)
    pack, far = pack_tile(
        info, window.transpose(0, 2, 1), kv, q, g, query_logsum, query_delta, piece
    )
    text = text_whole(piece)
    h1, h2 = swapped(pack, "height")
    t1, t2 = swapped(pack, "tm")

    terms = text_terms(info, pack, text, text_logsum, text_delta, far)
    parts = reduce_times(terms)
    sides = joined([h1, h2], terms)
    corner1, corner2 = swapped(sides, "tm")

    own = summed(parts, sides)
    own = exchange(own.transpose(1, 0, 2), "height")
    near = near_grads(pack, text, text_logsum, text_delta, (h1, h2, t1, t2), far)
    own = summed_heights(own, lax.axis_size("tm"), near)
    own = exchange(own, "tm")
    grad_q, grad_kv, done = far_grads(pack, corner1, corner2, far, near)
    text_grads = placed_rows(own, terms.shape[:3], done)
    return (
        grad_q.reshape(1, 1, tile, width),
        grad_kv.reshape(1, 1, 2, tile, width),
        text_grads,
    )


def solution(mesh):
    placed = (
        P("tm", "height", None, None),
        P("tm", "height", None, None),
        P("tm", "height", None, None, None),
        P("tm", "height", None, None),
        P("tm", "height", None, None),
        P(),
        P(None, "height", None),
        P("height", None),
        P(),
        P(),
        P(),
    )
    return jax.shard_map(
        on_device,
        mesh=mesh,
        in_specs=placed,
        out_specs=(
            P("tm", "height", None, None),
            P("tm", "height", None, None, None),
            P(None, "height", None),
        ),
        check_vma=False,
    )
```

```python
import functools

import jax
import jax.numpy as jnp
from jax import lax
from jax.experimental import pallas as pl
from jax.experimental.pallas import tpu as pltpu
from jax.sharding import PartitionSpec as P

HEAD = 128
GROUP = 3
WIDE = HEAD * GROUP
STEPS = 4
STAT_ROWS = 16
FAR = 1e30
SCALE = HEAD**-0.5
LOG2E = 1.4426950408889634
SCORE = SCALE * LOG2E
VMEM_LIMIT = 12 * 1024 * 1024
F32 = jnp.float32
BF16 = jnp.bfloat16


def nt(a, b):
    return lax.dot_general(a, b, (((1,), (1,)), ((), ())), preferred_element_type=F32)


def nn(a, b):
    return lax.dot_general(a, b, (((1,), (0,)), ((), ())), preferred_element_type=F32)


def lanes(i):
    return slice(i * HEAD, (i + 1) * HEAD)


def column(row):
    return jnp.broadcast_to(row, (HEAD, row.shape[1])).T


def pair(a, b):
    return jnp.concatenate([a, b], axis=0)


def wide(a, b):
    return jnp.concatenate([a, b], axis=1)


def query_scores(q, g, parts):
    return [(nt(q, k), nt(g, v)) for k, v, _ in parts]


def query_sum(scores, lse, delta, parts):
    grads = []
    for (s, w), (_, _, far) in zip(scores, parts):
        at = [x if x.shape[1] == s.shape[1] else wide(x, x) for x in (lse, delta)]
        p = jnp.exp2(s * SCORE - far - at[0])
        grads.append((p * (w - at[1])).astype(BF16))
    return functools.reduce(jnp.add, [nn(d, k) for d, (k, _, _) in zip(grads, parts)])


def key_scores(k, v, parts):
    return [(nt(k, q), nt(v, g)) for q, g, _, _ in parts]


def key_sums(scores, parts):
    grads = []
    for (s, w), (_, _, lse, delta) in zip(scores, parts):
        p = jnp.exp2(s * SCORE - lse)
        grads.append(((p * (w - delta)).astype(BF16), p.astype(BF16)))
    dk = functools.reduce(jnp.add, [nn(d, q) for (d, _), (q, _, _, _) in zip(grads, parts)])
    dv = functools.reduce(jnp.add, [nn(p, g) for (_, p), (_, g, _, _) in zip(grads, parts)])
    return dk, dv


def staggered(start, finish):
    held = start(0)
    for i in range(GROUP):
        later = start(i + 1) if i + 1 < GROUP else None
        finish(i, held)
        held = later


def call(body, name, ins, outs, out_shape, scratch=(), flops=0, bytes_accessed=0, exps=0):
    return pl.pallas_call(
        body,
        name=name,
        grid=(STEPS,),
        in_specs=ins,
        out_specs=outs,
        out_shape=out_shape,
        scratch_shapes=list(scratch),
        compiler_params=pltpu.CompilerParams(vmem_limit_bytes=VMEM_LIMIT),
        cost_estimate=pl.CostEstimate(
            flops=flops, bytes_accessed=bytes_accessed, transcendentals=exps
        ),
    )


def rows_spec(rows):
    return pl.BlockSpec((rows, WIDE), lambda j: (0, j))


def whole_spec(*shape):
    return pl.BlockSpec(shape, lambda j: (0,) * len(shape))


SCALARS = pl.BlockSpec(memory_space=pltpu.SMEM)
ANYWHERE = pl.BlockSpec(memory_space=pl.ANY)
TEXT_SPEC = pl.BlockSpec((4, 1, HEAD, WIDE), lambda j: (0, j >> 1, 0, j & 1))
NEAR_TIMES = 8
TILE = HEAD
PACK_ROWS = 4 * TILE + STAT_ROWS
FAR_ROWS = 32
OWN, H1, H2, T1, T2, T1H1, T1H2, T2H1, T2H2, TEXT_PLACE = range(10)
QUERY_PLACES = 16


def pack_tile(info, window, kv, q, g, lse, delta, earlier):
    times, _, heights = window.shape
    text_rows = HEAD

    heads = lse.shape[2]

    def body(info_ref, win_ref, kv_ref, q_ref, g_ref, l_ref, d_ref, _, o_ref, far_ref, slab_ref, sems):
        moves = [
            pltpu.make_async_copy(kv_ref, o_ref.at[0 : 2 * TILE], sems.at[0]),
            pltpu.make_async_copy(q_ref, o_ref.at[2 * TILE : 3 * TILE], sems.at[1]),
            pltpu.make_async_copy(g_ref, o_ref.at[3 * TILE : 4 * TILE], sems.at[2]),
        ]
        for move in moves:
            move.start()
        row = lax.broadcasted_iota(jnp.int32, (STAT_ROWS, HEAD), 0)
        for i in range(heads):
            slab = jnp.zeros((STAT_ROWS, HEAD), F32)
            at = 0
            for rest in (l_ref[0, 0, i : i + 1, :] * LOG2E, d_ref[0, 0, i : i + 1, :]):
                for _ in range(3):
                    part = rest.astype(BF16).astype(F32)
                    slab = jnp.where(row == at, part, slab)
                    rest = rest - part
                    at += 1
            slab_ref[:, lanes(i)] = slab.astype(BF16)
        last = pltpu.make_async_copy(slab_ref, o_ref.at[4 * TILE : PACK_ROWS], sems.at[3])
        last.start()

        t, h = info_ref[0], info_ref[1]
        a1, b1 = 1 - 2 * (t & 1), 1 - 2 * (h & 1)

        def sees(at_t, at_h, a, b):
            reach = [win_ref[at_t, n, at_h] for n in range(4)]
            return (a >= -reach[0]) & (a <= reach[1]) & (b >= -reach[2]) & (b <= reach[3])

        far_ref[...] = jnp.full((FAR_ROWS, HEAD), FAR, F32)
        places = ((0, 0), (0, b1), (0, -b1), (a1, 0), (-a1, 0))
        places += ((a1, b1), (a1, -b1), (-a1, b1), (-a1, -b1))
        for n, (a, b) in enumerate(places):
            at_t, at_h = t + a, h + b
            inside = (at_t >= 0) & (at_t < times) & (at_h >= 0) & (at_h < heights)
            at_t = jnp.clip(at_t, 0, times - 1)
            at_h = jnp.clip(at_h, 0, heights - 1)
            key = jnp.where(inside & sees(t, h, a, b), 0.0, FAR)
            query = jnp.where(inside & sees(at_t, at_h, -a, -b), 0.0, FAR)
            far_ref[n : n + 1, :] = jnp.full((1, HEAD), key, F32)
            far_ref[QUERY_PLACES + n : QUERY_PLACES + n + 1, :] = jnp.full((1, HEAD), query, F32)
        slot = lax.broadcasted_iota(jnp.int32, (1, text_rows), 1)
        text = jnp.where(slot < info_ref[2], 0.0, FAR)
        far_ref[TEXT_PLACE : TEXT_PLACE + 1, :] = text
        far_ref[QUERY_PLACES + TEXT_PLACE : QUERY_PLACES + TEXT_PLACE + 1, :] = text

        for move in moves:
            move.wait()
        last.wait()

    vmem = pl.BlockSpec(memory_space=pltpu.VMEM)
    return pl.pallas_call(
        body,
        name="pack_tile",
        in_specs=[SCALARS, SCALARS, ANYWHERE, ANYWHERE, ANYWHERE, vmem, vmem, ANYWHERE],
        out_specs=[ANYWHERE, vmem],
        out_shape=[
            jax.ShapeDtypeStruct((PACK_ROWS, q.shape[1]), BF16),
            jax.ShapeDtypeStruct((FAR_ROWS, HEAD), F32),
        ],
        scratch_shapes=[
            pltpu.VMEM((STAT_ROWS, q.shape[1]), BF16),
            pltpu.SemaphoreType.DMA((4,)),
        ],
        compiler_params=pltpu.CompilerParams(vmem_limit_bytes=VMEM_LIMIT),
        cost_estimate=pl.CostEstimate(
            flops=0, bytes_accessed=8 * TILE * q.shape[1] * 2, transcendentals=0
        ),
    )(info, window, kv, q, g, lse, delta, earlier)


def joined(arrays, *earlier):
    count = len(arrays)

    def body(*refs):
        o_ref = refs[-1]
        for n in range(count):
            o_ref[n] = refs[n][...]

    rows, width = arrays[0].shape
    return call(
        body,
        "joined",
        [rows_spec(rows)] * count + [ANYWHERE] * len(earlier),
        pl.BlockSpec((count, rows, WIDE), lambda j: (0, 0, j)),
        jax.ShapeDtypeStruct((count, rows, width), BF16),
        bytes_accessed=4 * count * rows * width,
    )(*arrays, *earlier)


def keys_of(ref, at):
    return ref[0:TILE, at], ref[TILE : 2 * TILE, at]


def queries_of(ref, at):
    return ref[2 * TILE : 3 * TILE, at], ref[3 * TILE : 4 * TILE, at]


def stats_of(ref, at):
    slab = ref[4 * TILE :, at].astype(F32)
    lse = (slab[0:1] + slab[1:2]) + slab[2:3]
    delta = (slab[3:4] + slab[4:5]) + slab[5:6]
    return lse, delta


def far_of(far_ref, place, queries=False):
    row = place + (QUERY_PLACES if queries else 0)
    return far_ref[row : row + 1, :]


def key_pair(one, other):
    return pair(one[0], other[0]), pair(one[1], other[1]), wide(one[2], other[2])


def query_pair(one, other):
    return (
        pair(one[0], other[0]),
        pair(one[1], other[1]),
        wide(one[2], other[2]),
        wide(one[3], other[3]),
    )


def text_terms(info, pack, text, text_lse, text_delta, far):
    def body(info_ref, pack_ref, text_ref, tl_ref, td_ref, far_ref, o_ref, sum_ref):
        step = pl.program_id(0)
        linear = info_ref[3]
        row = lax.broadcasted_iota(jnp.int32, (HEAD, HEAD), 0)
        valid = row < info_ref[2]
        none = jnp.zeros((1, HEAD), F32)
        work = []
        for i in range(GROUP):
            at = lanes(i)
            which = pl.ds(step * GROUP + i, 1)
            tq, tk, tv, tg = (text_ref[n, 0, :, at] for n in range(4))
            lse, delta = tl_ref[which, :] * LOG2E, td_ref[which, :]
            work.append((tq, tk, tv, tg, lse, delta, column(lse), column(delta)))

        def start(i):
            at = lanes(i)
            tq, tk, tv, tg = work[i][:4]
            keys = [(*keys_of(pack_ref, at), none)]
            mine = [(*queries_of(pack_ref, at), *stats_of(pack_ref, at))]
            return query_scores(tq, tg, keys), keys, key_scores(tk, tv, mine), mine

        def finish(i, held):
            query, keys, key, mine = held
            sum_ref[i, 0] = query_sum(query, work[i][6], work[i][7], keys)
            sum_ref[i, 1], sum_ref[i, 2] = key_sums(key, mine)

        staggered(start, finish)
        for i in range(GROUP):
            tq, tk, tv, tg, lse, delta, lse_rows, delta_rows = work[i]

            @pl.when(linear == step * GROUP + i)
            def _():
                keys = [(tk, tv, far_of(far_ref, TEXT_PLACE))]
                sum_ref[i, 0] += query_sum(query_scores(tq, tg, keys), lse_rows, delta_rows, keys)
                mine = [(tq, tg, lse + far_of(far_ref, TEXT_PLACE, True), delta)]
                dk, dv = key_sums(key_scores(tk, tv, mine), mine)
                sum_ref[i, 1] += dk
                sum_ref[i, 2] += dv

        for i in range(GROUP):
            for n in range(3):
                total = sum_ref[i, n]
                total = total * SCALE if n < 2 else total
                sum_ref[i, n] = jnp.where(valid, total, 0.0)
                for r in range(4):
                    o_ref[r, n, i] = sum_ref[i, n, pl.ds(r, 32, stride=4), :].astype(BF16)

    heads = text_lse.shape[0]
    return call(
        body,
        "text_terms",
        [SCALARS, rows_spec(PACK_ROWS), TEXT_SPEC]
        + [whole_spec(heads, HEAD)] * 2
        + [whole_spec(FAR_ROWS, HEAD)],
        pl.BlockSpec((4, 3, GROUP, 32, HEAD), lambda j: (0, 0, j, 0, 0)),
        jax.ShapeDtypeStruct((4, 3, STEPS * GROUP, 32, HEAD), BF16),
        scratch=[pltpu.VMEM((GROUP, 3, HEAD, HEAD), F32)],
        flops=7 * 12 * 2 * 128**3,
        bytes_accessed=4_400_000,
        exps=2 * 12 * 128 * 128,
    )(info, pack, text, text_lse, text_delta, far)


def near_grads(pack, text, text_lse, text_delta, places, far):
    def body(p_ref, text_ref, tl_ref, td_ref, h1_ref, h2_ref, t1_ref, t2_ref, far_ref, o_ref):
        step = pl.program_id(0)

        def start(i):
            at = lanes(i)
            which = pl.ds(step * GROUP + i, 1)
            q, g = queries_of(p_ref, at)
            k, v = keys_of(p_ref, at)

            def key(ref, place):
                return (*keys_of(ref, at), far_of(far_ref, place))

            def query(ref, place):
                more, d = stats_of(ref, at)
                return (*queries_of(ref, at), more + far_of(far_ref, place, True), d)

            text_key = (text_ref[1, 0, :, at], text_ref[2, 0, :, at], far_of(far_ref, TEXT_PLACE))
            text_query = (
                text_ref[0, 0, :, at],
                text_ref[3, 0, :, at],
                tl_ref[which, :] * LOG2E + far_of(far_ref, TEXT_PLACE, True),
                td_ref[which, :],
            )
            keys = [
                key_pair(key(p_ref, OWN), text_key),
                key_pair(key(h1_ref, H1), key(h2_ref, H2)),
                key_pair(key(t1_ref, T1), key(t2_ref, T2)),
            ]
            mine = [
                query_pair(query(p_ref, OWN), text_query),
                query_pair(query(h1_ref, H1), query(h2_ref, H2)),
                query_pair(query(t1_ref, T1), query(t2_ref, T2)),
            ]
            return query_scores(q, g, keys), keys, key_scores(k, v, mine), mine

        def finish(i, held):
            at = lanes(i)
            query, keys, key, mine = held
            lse, delta = stats_of(p_ref, at)
            o_ref[0:TILE, at] = query_sum(query, column(lse), column(delta), keys)
            o_ref[TILE : 2 * TILE, at], o_ref[2 * TILE : 3 * TILE, at] = key_sums(key, mine)

        staggered(start, finish)

    heads = text_lse.shape[0]
    return call(
        body,
        "near_grads",
        [rows_spec(PACK_ROWS), TEXT_SPEC]
        + [whole_spec(heads, HEAD)] * 2
        + [rows_spec(PACK_ROWS)] * 4
        + [whole_spec(FAR_ROWS, HEAD)],
        rows_spec(3 * TILE),
        jax.ShapeDtypeStruct((3 * TILE, pack.shape[1]), F32),
        flops=42 * 12 * 2 * 128**3,
        bytes_accessed=12_000_000,
        exps=12 * 12 * 128 * 128,
    )(pack, text, text_lse, text_delta, *places, far)


def far_grads(pack, corner1, corner2, far, near):
    def body(p_ref, c1_ref, c2_ref, far_ref, near_ref, q_ref, kv_ref, done_ref):
        done_ref[...] = far_ref[0:8, :]
        refs = (
            ((c1_ref.at[0], T1H1), (c1_ref.at[1], T1H2)),
            ((c2_ref.at[0], T2H1), (c2_ref.at[1], T2H2)),
        )

        def start(i):
            at = lanes(i)
            q, g = queries_of(p_ref, at)
            k, v = keys_of(p_ref, at)

            def key(ref, place):
                return (*keys_of(ref, at), far_of(far_ref, place))

            def query(ref, place):
                more, d = stats_of(ref, at)
                return (*queries_of(ref, at), more + far_of(far_ref, place, True), d)

            keys = [key_pair(key(*one), key(*other)) for one, other in refs]
            mine = [query_pair(query(*one), query(*other)) for one, other in refs]
            return query_scores(q, g, keys), keys, key_scores(k, v, mine), mine

        def finish(i, held):
            at = lanes(i)
            query, keys, key, mine = held
            lse, delta = stats_of(p_ref, at)
            dq = near_ref[0:TILE, at] + query_sum(query, column(lse), column(delta), keys)
            dk, dv = key_sums(key, mine)
            q_ref[:, at] = (dq * SCALE).astype(BF16)
            kv_ref[0:TILE, at] = ((near_ref[TILE : 2 * TILE, at] + dk) * SCALE).astype(BF16)
            kv_ref[TILE : 2 * TILE, at] = (near_ref[2 * TILE : 3 * TILE, at] + dv).astype(BF16)

        staggered(start, finish)

    two = pl.BlockSpec((2, PACK_ROWS, WIDE), lambda j: (0, 0, j))
    width = pack.shape[1]
    return call(
        body,
        "far_grads",
        [rows_spec(PACK_ROWS), two, two, whole_spec(FAR_ROWS, HEAD), rows_spec(3 * TILE)],
        [rows_spec(TILE), rows_spec(2 * TILE), whole_spec(8, HEAD)],
        [
            jax.ShapeDtypeStruct((TILE, width), BF16),
            jax.ShapeDtypeStruct((2 * TILE, width), BF16),
            jax.ShapeDtypeStruct((8, HEAD), F32),
        ],
        flops=28 * 12 * 2 * 128**3,
        bytes_accessed=12_000_000,
        exps=8 * 12 * 128 * 128,
    )(pack, corner1, corner2, far, near)


def swapped(array, axis):
    count = lax.axis_size(axis)
    both = []
    for first in (0, 1):
        pairs = []
        for i in range(first, count - 1, 2):
            pairs += [(i, i + 1), (i + 1, i)]
        both.append(lax.ppermute(array, axis, pairs))
    return both


def exchange(array, axis, group=None):
    count = lax.axis_size(axis)
    runs = None
    if group is not None:
        runs = [list(range(i, i + group)) for i in range(0, count, group)]
    return lax.all_to_all(array, axis, 0, 0, axis_index_groups=runs, tiled=True)


def text_piece(text_inputs, text_grad_out):
    place = lax.axis_index("tm") & (NEAR_TIMES - 1)
    heights = lax.axis_size("height")
    share, width = text_grad_out.shape
    text = jnp.concatenate([text_inputs, text_grad_out[None]], axis=0)
    start = (place >> 1, 0, (place & 1) * (width // 2))
    piece = lax.dynamic_slice(text, start, (1, share, width // 2))
    rows = exchange(jnp.broadcast_to(piece, (heights, share, width // 2)), "height")
    return rows.reshape(1, share * heights, width // 2)


def text_whole(rows):
    full = exchange(jnp.broadcast_to(rows, (NEAR_TIMES, *rows.shape[1:])), "tm", NEAR_TIMES)
    return full.reshape(4, 2, *rows.shape[1:])


def reduce_times(terms):
    heights, lane = terms.shape[3:]
    return exchange(terms.reshape(NEAR_TIMES, -1, heights, lane), "tm", NEAR_TIMES)


def small(body, name, out_shape, array, earlier):
    return pl.pallas_call(
        body,
        name=name,
        in_specs=[pl.BlockSpec(memory_space=pltpu.VMEM), ANYWHERE],
        out_specs=pl.BlockSpec(memory_space=pltpu.VMEM),
        out_shape=out_shape,
        compiler_params=pltpu.CompilerParams(vmem_limit_bytes=VMEM_LIMIT),
        cost_estimate=pl.CostEstimate(flops=0, bytes_accessed=1_500_000, transcendentals=0),
    )(array, earlier)


def summed(parts, earlier):
    shape = parts.shape[1:]

    def body(p_ref, _, o_ref):
        for u in range(shape[0]):
            total = p_ref[0, u].astype(F32)
            for n in range(1, parts.shape[0]):
                total += p_ref[n, u].astype(F32)
            o_ref[u] = total.astype(BF16)

    return small(body, "summed", jax.ShapeDtypeStruct(shape, BF16), parts, earlier)


def summed_heights(parts, copies, earlier):
    count, units, lane = parts.shape

    def body(p_ref, _, o_ref):
        total = p_ref[0].astype(F32)
        for n in range(1, count):
            total += p_ref[n].astype(F32)
        for n in range(copies):
            o_ref[n] = total

    shape = jax.ShapeDtypeStruct((copies, units, lane), F32)
    return small(body, "summed_heights", shape, parts, earlier)


def placed_rows(parts, shape, earlier):
    share, kinds, heads = shape
    members, units, lane = parts.shape
    places = units * NEAR_TIMES // share

    def body(p_ref, _, o_ref):
        for place in range(NEAR_TIMES):
            total = p_ref[place]
            for run in range(1, members // NEAR_TIMES):
                total += p_ref[run * NEAR_TIMES + place]
            for u in range(units):
                at = place * units + u
                row, unit = at // places, at % places
                o_ref[unit // heads, row : row + 1, lanes(unit % heads)] = total[u : u + 1]

    out = jax.ShapeDtypeStruct((kinds, share, heads * lane), F32)
    return small(body, "placed_rows", out, parts, earlier)


def on_device(
    queries,
    grad_out,
    key_value,
    query_logsum,
    query_delta,
    window,
    text_inputs,
    text_grad_out,
    text_logsum,
    text_delta,
    text_length,
):
    t, h = lax.axis_index("tm"), lax.axis_index("height")
    heights = lax.axis_size("height")
    tile, width = queries.shape[2:]

    q = queries.reshape(tile, width)
    g = grad_out.reshape(tile, width)
    kv = key_value.reshape(2 * tile, width)
    info = jnp.stack([t, h, text_length[0], t * heights + h]).astype(jnp.int32)

    piece = text_piece(text_inputs, text_grad_out)
    pack, far = pack_tile(
        info, window.transpose(0, 2, 1), kv, q, g, query_logsum, query_delta, piece
    )
    text = text_whole(piece)
    h1, h2 = swapped(pack, "height")
    t1, t2 = swapped(pack, "tm")

    terms = text_terms(info, pack, text, text_logsum, text_delta, far)
    parts = reduce_times(terms)
    sides = joined([h1, h2], t1, t2, parts)
    corner1, corner2 = swapped(sides, "tm")

    own = summed(parts, sides)
    own = exchange(own.transpose(1, 0, 2), "height")
    near = near_grads(pack, text, text_logsum, text_delta, (h1, h2, t1, t2), far)
    own = summed_heights(own, lax.axis_size("tm"), near)
    own = exchange(own, "tm")
    grad_q, grad_kv, done = far_grads(pack, corner1, corner2, far, near)
    text_grads = placed_rows(own, terms.shape[:3], done)
    return (
        grad_q.reshape(1, 1, tile, width),
        grad_kv.reshape(1, 1, 2, tile, width),
        text_grads,
    )


def solution(mesh):
    placed = (
        P("tm", "height", None, None),
        P("tm", "height", None, None),
        P("tm", "height", None, None, None),
        P("tm", "height", None, None),
        P("tm", "height", None, None),
        P(),
        P(None, "height", None),
        P("height", None),
        P(),
        P(),
        P(),
    )
    return jax.shard_map(
        on_device,
        mesh=mesh,
        in_specs=placed,
        out_specs=(
            P("tm", "height", None, None),
            P("tm", "height", None, None, None),
            P(None, "height", None),
        ),
        check_vma=False,
    )
```

```python
import functools

import jax
import jax.numpy as jnp
from jax import lax
from jax.experimental import pallas as pl
from jax.experimental.pallas import tpu as pltpu
from jax.sharding import PartitionSpec as P

HEAD = 128
GROUP = 3
WIDE = HEAD * GROUP
STEPS = 4
STAT_ROWS = 16
FAR = 1e30
SCALE = HEAD**-0.5
LOG2E = 1.4426950408889634
SCORE = SCALE * LOG2E
VMEM_LIMIT = 12 * 1024 * 1024
F32 = jnp.float32
BF16 = jnp.bfloat16


def nt(a, b):
    return lax.dot_general(a, b, (((1,), (1,)), ((), ())), preferred_element_type=F32)


def nn(a, b):
    return lax.dot_general(a, b, (((1,), (0,)), ((), ())), preferred_element_type=F32)


def lanes(i):
    return slice(i * HEAD, (i + 1) * HEAD)


def column(row):
    return jnp.broadcast_to(row, (HEAD, row.shape[1])).T


def pair(a, b):
    return jnp.concatenate([a, b], axis=0)


def wide(a, b):
    return jnp.concatenate([a, b], axis=1)


def query_scores(q, g, parts):
    return [(nt(q, k), nt(g, v)) for k, v, _ in parts]


def query_sum(scores, lse, delta, parts):
    grads = []
    for (s, w), (_, _, far) in zip(scores, parts):
        at = [x if x.shape[1] == s.shape[1] else wide(x, x) for x in (lse, delta)]
        p = jnp.exp2(s * SCORE - far - at[0])
        grads.append((p * (w - at[1])).astype(BF16))
    return functools.reduce(jnp.add, [nn(d, k) for d, (k, _, _) in zip(grads, parts)])


def key_scores(k, v, parts):
    return [(nt(k, q), nt(v, g)) for q, g, _, _ in parts]


def key_sums(scores, parts):
    grads = []
    for (s, w), (_, _, lse, delta) in zip(scores, parts):
        p = jnp.exp2(s * SCORE - lse)
        grads.append(((p * (w - delta)).astype(BF16), p.astype(BF16)))
    dk = functools.reduce(jnp.add, [nn(d, q) for (d, _), (q, _, _, _) in zip(grads, parts)])
    dv = functools.reduce(jnp.add, [nn(p, g) for (_, p), (_, g, _, _) in zip(grads, parts)])
    return dk, dv


def staggered(start, finish):
    held = start(0)
    for i in range(GROUP):
        later = start(i + 1) if i + 1 < GROUP else None
        finish(i, held)
        held = later


def call(body, name, ins, outs, out_shape, scratch=(), flops=0, bytes_accessed=0, exps=0):
    return pl.pallas_call(
        body,
        name=name,
        grid=(STEPS,),
        in_specs=ins,
        out_specs=outs,
        out_shape=out_shape,
        scratch_shapes=list(scratch),
        compiler_params=pltpu.CompilerParams(vmem_limit_bytes=VMEM_LIMIT),
        cost_estimate=pl.CostEstimate(
            flops=flops, bytes_accessed=bytes_accessed, transcendentals=exps
        ),
    )


def rows_spec(rows):
    return pl.BlockSpec((rows, WIDE), lambda j: (0, j))


def whole_spec(*shape):
    return pl.BlockSpec(shape, lambda j: (0,) * len(shape))


SCALARS = pl.BlockSpec(memory_space=pltpu.SMEM)
ANYWHERE = pl.BlockSpec(memory_space=pl.ANY)
TEXT_SPEC = pl.BlockSpec((4, 1, HEAD, WIDE), lambda j: (0, j >> 1, 0, j & 1))
NEAR_TIMES = 8
TILE = HEAD
PACK_ROWS = 4 * TILE + STAT_ROWS
FAR_ROWS = 32
OWN, H1, H2, T1, T2, T1H1, T1H2, T2H1, T2H2, TEXT_PLACE = range(10)
QUERY_PLACES = 16


def pack_tile(info, window, kv, q, g, lse, delta, earlier):
    times, _, heights = window.shape
    text_rows = HEAD

    heads = lse.shape[2]

    def body(info_ref, win_ref, kv_ref, q_ref, g_ref, l_ref, d_ref, _, o_ref, far_ref, slab_ref, sems):
        moves = [
            pltpu.make_async_copy(kv_ref, o_ref.at[0 : 2 * TILE], sems.at[0]),
            pltpu.make_async_copy(q_ref, o_ref.at[2 * TILE : 3 * TILE], sems.at[1]),
            pltpu.make_async_copy(g_ref, o_ref.at[3 * TILE : 4 * TILE], sems.at[2]),
        ]
        for move in moves:
            move.start()
        row = lax.broadcasted_iota(jnp.int32, (STAT_ROWS, HEAD), 0)
        for i in range(heads):
            slab = jnp.zeros((STAT_ROWS, HEAD), F32)
            at = 0
            for rest in (l_ref[0, 0, i : i + 1, :] * LOG2E, d_ref[0, 0, i : i + 1, :]):
                for _ in range(3):
                    part = rest.astype(BF16).astype(F32)
                    slab = jnp.where(row == at, part, slab)
                    rest = rest - part
                    at += 1
            slab_ref[:, lanes(i)] = slab.astype(BF16)
        last = pltpu.make_async_copy(slab_ref, o_ref.at[4 * TILE : PACK_ROWS], sems.at[3])
        last.start()

        t, h = info_ref[0], info_ref[1]
        a1, b1 = 1 - 2 * (t & 1), 1 - 2 * (h & 1)

        def sees(at_t, at_h, a, b):
            reach = [win_ref[at_t, n, at_h] for n in range(4)]
            return (a >= -reach[0]) & (a <= reach[1]) & (b >= -reach[2]) & (b <= reach[3])

        far_ref[...] = jnp.full((FAR_ROWS, HEAD), FAR, F32)
        places = ((0, 0), (0, b1), (0, -b1), (a1, 0), (-a1, 0))
        places += ((a1, b1), (a1, -b1), (-a1, b1), (-a1, -b1))
        for n, (a, b) in enumerate(places):
            at_t, at_h = t + a, h + b
            inside = (at_t >= 0) & (at_t < times) & (at_h >= 0) & (at_h < heights)
            at_t = jnp.clip(at_t, 0, times - 1)
            at_h = jnp.clip(at_h, 0, heights - 1)
            key = jnp.where(inside & sees(t, h, a, b), 0.0, FAR)
            query = jnp.where(inside & sees(at_t, at_h, -a, -b), 0.0, FAR)
            far_ref[n : n + 1, :] = jnp.full((1, HEAD), key, F32)
            far_ref[QUERY_PLACES + n : QUERY_PLACES + n + 1, :] = jnp.full((1, HEAD), query, F32)
        slot = lax.broadcasted_iota(jnp.int32, (1, text_rows), 1)
        text = jnp.where(slot < info_ref[2], 0.0, FAR)
        far_ref[TEXT_PLACE : TEXT_PLACE + 1, :] = text
        far_ref[QUERY_PLACES + TEXT_PLACE : QUERY_PLACES + TEXT_PLACE + 1, :] = text

        for move in moves:
            move.wait()
        last.wait()

    vmem = pl.BlockSpec(memory_space=pltpu.VMEM)
    return pl.pallas_call(
        body,
        name="pack_tile",
        in_specs=[SCALARS, SCALARS, ANYWHERE, ANYWHERE, ANYWHERE, vmem, vmem, ANYWHERE],
        out_specs=[ANYWHERE, vmem],
        out_shape=[
            jax.ShapeDtypeStruct((PACK_ROWS, q.shape[1]), BF16),
            jax.ShapeDtypeStruct((FAR_ROWS, HEAD), F32),
        ],
        scratch_shapes=[
            pltpu.VMEM((STAT_ROWS, q.shape[1]), BF16),
            pltpu.SemaphoreType.DMA((4,)),
        ],
        compiler_params=pltpu.CompilerParams(vmem_limit_bytes=VMEM_LIMIT),
        cost_estimate=pl.CostEstimate(
            flops=0, bytes_accessed=8 * TILE * q.shape[1] * 2, transcendentals=0
        ),
    )(info, window, kv, q, g, lse, delta, earlier)


def joined(arrays, *earlier):
    count = len(arrays)

    def body(*refs):
        o_ref = refs[-1]
        for n in range(count):
            o_ref[n] = refs[n][...]

    rows, width = arrays[0].shape
    return call(
        body,
        "joined",
        [rows_spec(rows)] * count + [ANYWHERE] * len(earlier),
        pl.BlockSpec((count, rows, WIDE), lambda j: (0, 0, j)),
        jax.ShapeDtypeStruct((count, rows, width), BF16),
        bytes_accessed=4 * count * rows * width,
    )(*arrays, *earlier)


def keys_of(ref, at):
    return ref[0:TILE, at], ref[TILE : 2 * TILE, at]


def queries_of(ref, at):
    return ref[2 * TILE : 3 * TILE, at], ref[3 * TILE : 4 * TILE, at]


def stats_of(ref, at):
    slab = ref[4 * TILE :, at].astype(F32)
    lse = (slab[0:1] + slab[1:2]) + slab[2:3]
    delta = (slab[3:4] + slab[4:5]) + slab[5:6]
    return lse, delta


def far_of(far_ref, place, queries=False):
    row = place + (QUERY_PLACES if queries else 0)
    return far_ref[row : row + 1, :]


def key_pair(one, other):
    return pair(one[0], other[0]), pair(one[1], other[1]), wide(one[2], other[2])


def query_pair(one, other):
    return (
        pair(one[0], other[0]),
        pair(one[1], other[1]),
        wide(one[2], other[2]),
        wide(one[3], other[3]),
    )


def text_terms(info, pack, text, text_lse, text_delta, far):
    def body(info_ref, pack_ref, text_ref, tl_ref, td_ref, far_ref, o_ref, sum_ref):
        step = pl.program_id(0)
        linear = info_ref[3]
        row = lax.broadcasted_iota(jnp.int32, (HEAD, HEAD), 0)
        valid = row < info_ref[2]
        none = jnp.zeros((1, HEAD), F32)
        work = []
        for i in range(GROUP):
            at = lanes(i)
            which = pl.ds(step * GROUP + i, 1)
            tq, tk, tv, tg = (text_ref[n, 0, :, at] for n in range(4))
            lse, delta = tl_ref[which, :] * LOG2E, td_ref[which, :]
            work.append((tq, tk, tv, tg, lse, delta, column(lse), column(delta)))

        def start(i):
            at = lanes(i)
            tq, tk, tv, tg = work[i][:4]
            keys = [(*keys_of(pack_ref, at), none)]
            mine = [(*queries_of(pack_ref, at), *stats_of(pack_ref, at))]
            return query_scores(tq, tg, keys), keys, key_scores(tk, tv, mine), mine

        def finish(i, held):
            query, keys, key, mine = held
            sum_ref[i, 0] = query_sum(query, work[i][6], work[i][7], keys)
            sum_ref[i, 1], sum_ref[i, 2] = key_sums(key, mine)

        staggered(start, finish)
        for i in range(GROUP):
            tq, tk, tv, tg, lse, delta, lse_rows, delta_rows = work[i]

            @pl.when(linear == step * GROUP + i)
            def _():
                keys = [(tk, tv, far_of(far_ref, TEXT_PLACE))]
                sum_ref[i, 0] += query_sum(query_scores(tq, tg, keys), lse_rows, delta_rows, keys)
                mine = [(tq, tg, lse + far_of(far_ref, TEXT_PLACE, True), delta)]
                dk, dv = key_sums(key_scores(tk, tv, mine), mine)
                sum_ref[i, 1] += dk
                sum_ref[i, 2] += dv

        for i in range(GROUP):
            for n in range(3):
                total = sum_ref[i, n]
                total = total * SCALE if n < 2 else total
                sum_ref[i, n] = jnp.where(valid, total, 0.0)
                for r in range(4):
                    o_ref[r, n, i] = sum_ref[i, n, pl.ds(r, 32, stride=4), :].astype(BF16)

    heads = text_lse.shape[0]
    return call(
        body,
        "text_terms",
        [SCALARS, rows_spec(PACK_ROWS), TEXT_SPEC]
        + [whole_spec(heads, HEAD)] * 2
        + [whole_spec(FAR_ROWS, HEAD)],
        pl.BlockSpec((4, 3, GROUP, 32, HEAD), lambda j: (0, 0, j, 0, 0)),
        jax.ShapeDtypeStruct((4, 3, STEPS * GROUP, 32, HEAD), BF16),
        scratch=[pltpu.VMEM((GROUP, 3, HEAD, HEAD), F32)],
        flops=7 * 12 * 2 * 128**3,
        bytes_accessed=4_400_000,
        exps=2 * 12 * 128 * 128,
    )(info, pack, text, text_lse, text_delta, far)


def near_grads(pack, text, text_lse, text_delta, places, far):
    def body(p_ref, text_ref, tl_ref, td_ref, h1_ref, h2_ref, t1_ref, t2_ref, far_ref, o_ref):
        step = pl.program_id(0)

        def start(i):
            at = lanes(i)
            which = pl.ds(step * GROUP + i, 1)
            q, g = queries_of(p_ref, at)
            k, v = keys_of(p_ref, at)

            def key(ref, place):
                return (*keys_of(ref, at), far_of(far_ref, place))

            def query(ref, place):
                more, d = stats_of(ref, at)
                return (*queries_of(ref, at), more + far_of(far_ref, place, True), d)

            text_key = (text_ref[1, 0, :, at], text_ref[2, 0, :, at], far_of(far_ref, TEXT_PLACE))
            text_query = (
                text_ref[0, 0, :, at],
                text_ref[3, 0, :, at],
                tl_ref[which, :] * LOG2E + far_of(far_ref, TEXT_PLACE, True),
                td_ref[which, :],
            )
            keys = [
                key_pair(key(p_ref, OWN), text_key),
                key_pair(key(h1_ref, H1), key(h2_ref, H2)),
                key_pair(key(t1_ref, T1), key(t2_ref, T2)),
            ]
            mine = [
                query_pair(query(p_ref, OWN), text_query),
                query_pair(query(h1_ref, H1), query(h2_ref, H2)),
                query_pair(query(t1_ref, T1), query(t2_ref, T2)),
            ]
            return query_scores(q, g, keys), keys, key_scores(k, v, mine), mine

        def finish(i, held):
            at = lanes(i)
            query, keys, key, mine = held
            lse, delta = stats_of(p_ref, at)
            o_ref[0:TILE, at] = query_sum(query, column(lse), column(delta), keys)
            o_ref[TILE : 2 * TILE, at], o_ref[2 * TILE : 3 * TILE, at] = key_sums(key, mine)

        staggered(start, finish)

    heads = text_lse.shape[0]
    return call(
        body,
        "near_grads",
        [rows_spec(PACK_ROWS), TEXT_SPEC]
        + [whole_spec(heads, HEAD)] * 2
        + [rows_spec(PACK_ROWS)] * 4
        + [whole_spec(FAR_ROWS, HEAD)],
        rows_spec(3 * TILE),
        jax.ShapeDtypeStruct((3 * TILE, pack.shape[1]), F32),
        flops=42 * 12 * 2 * 128**3,
        bytes_accessed=12_000_000,
        exps=12 * 12 * 128 * 128,
    )(pack, text, text_lse, text_delta, *places, far)


def far_grads(pack, corner1, corner2, far, near):
    def body(p_ref, c1_ref, c2_ref, far_ref, near_ref, q_ref, kv_ref, done_ref):
        done_ref[...] = far_ref[0:8, :]
        refs = (
            ((c1_ref.at[0], T1H1), (c1_ref.at[1], T1H2)),
            ((c2_ref.at[0], T2H1), (c2_ref.at[1], T2H2)),
        )

        def start(i):
            at = lanes(i)
            q, g = queries_of(p_ref, at)
            k, v = keys_of(p_ref, at)

            def key(ref, place):
                return (*keys_of(ref, at), far_of(far_ref, place))

            def query(ref, place):
                more, d = stats_of(ref, at)
                return (*queries_of(ref, at), more + far_of(far_ref, place, True), d)

            keys = [key_pair(key(*one), key(*other)) for one, other in refs]
            mine = [query_pair(query(*one), query(*other)) for one, other in refs]
            return query_scores(q, g, keys), keys, key_scores(k, v, mine), mine

        def finish(i, held):
            at = lanes(i)
            query, keys, key, mine = held
            lse, delta = stats_of(p_ref, at)
            dq = near_ref[0:TILE, at] + query_sum(query, column(lse), column(delta), keys)
            dk, dv = key_sums(key, mine)
            q_ref[:, at] = (dq * SCALE).astype(BF16)
            kv_ref[0:TILE, at] = ((near_ref[TILE : 2 * TILE, at] + dk) * SCALE).astype(BF16)
            kv_ref[TILE : 2 * TILE, at] = (near_ref[2 * TILE : 3 * TILE, at] + dv).astype(BF16)

        staggered(start, finish)

    two = pl.BlockSpec((2, PACK_ROWS, WIDE), lambda j: (0, 0, j))
    width = pack.shape[1]
    return call(
        body,
        "far_grads",
        [rows_spec(PACK_ROWS), two, two, whole_spec(FAR_ROWS, HEAD), rows_spec(3 * TILE)],
        [rows_spec(TILE), rows_spec(2 * TILE), whole_spec(8, HEAD)],
        [
            jax.ShapeDtypeStruct((TILE, width), BF16),
            jax.ShapeDtypeStruct((2 * TILE, width), BF16),
            jax.ShapeDtypeStruct((8, HEAD), F32),
        ],
        flops=28 * 12 * 2 * 128**3,
        bytes_accessed=12_000_000,
        exps=8 * 12 * 128 * 128,
    )(pack, corner1, corner2, far, near)


def swapped(array, axis):
    count = lax.axis_size(axis)
    both = []
    for first in (0, 1):
        pairs = []
        for i in range(first, count - 1, 2):
            pairs += [(i, i + 1), (i + 1, i)]
        both.append(lax.ppermute(array, axis, pairs))
    return both


def exchange(array, axis, group=None):
    count = lax.axis_size(axis)
    runs = None
    if group is not None:
        runs = [list(range(i, i + group)) for i in range(0, count, group)]
    return lax.all_to_all(array, axis, 0, 0, axis_index_groups=runs, tiled=True)


def text_piece(text_inputs, text_grad_out):
    place = lax.axis_index("tm") & (NEAR_TIMES - 1)
    heights = lax.axis_size("height")
    share, width = text_grad_out.shape
    text = jnp.concatenate([text_inputs, text_grad_out[None]], axis=0)
    start = (place >> 1, 0, (place & 1) * (width // 2))
    piece = lax.dynamic_slice(text, start, (1, share, width // 2))
    rows = exchange(jnp.broadcast_to(piece, (heights, share, width // 2)), "height")
    return rows.reshape(1, share * heights, width // 2)


def text_whole(rows):
    full = exchange(jnp.broadcast_to(rows, (NEAR_TIMES, *rows.shape[1:])), "tm", NEAR_TIMES)
    return full.reshape(4, 2, *rows.shape[1:])


def reduce_times(terms):
    heights, lane = terms.shape[3:]
    return exchange(terms.reshape(NEAR_TIMES, -1, heights, lane), "tm", NEAR_TIMES)


def small(body, name, out_shape, array, earlier):
    return pl.pallas_call(
        body,
        name=name,
        in_specs=[pl.BlockSpec(memory_space=pltpu.VMEM), ANYWHERE],
        out_specs=pl.BlockSpec(memory_space=pltpu.VMEM),
        out_shape=out_shape,
        compiler_params=pltpu.CompilerParams(vmem_limit_bytes=VMEM_LIMIT),
        cost_estimate=pl.CostEstimate(flops=0, bytes_accessed=1_500_000, transcendentals=0),
    )(array, earlier)


def summed(parts, earlier):
    shape = parts.shape[1:]

    def body(p_ref, _, o_ref):
        for u in range(shape[0]):
            total = p_ref[0, u].astype(F32)
            for n in range(1, parts.shape[0]):
                total += p_ref[n, u].astype(F32)
            o_ref[u] = total.astype(BF16)

    return small(body, "summed", jax.ShapeDtypeStruct(shape, BF16), parts, earlier)


def summed_heights(parts, copies, earlier):
    count, units, lane = parts.shape

    def body(p_ref, _, o_ref):
        total = p_ref[0].astype(F32)
        for n in range(1, count):
            total += p_ref[n].astype(F32)
        for n in range(copies):
            o_ref[n] = total

    shape = jax.ShapeDtypeStruct((copies, units, lane), F32)
    return small(body, "summed_heights", shape, parts, earlier)


def placed_rows(parts, shape, earlier):
    share, kinds, heads = shape
    members, units, lane = parts.shape
    places = units * NEAR_TIMES // share

    def body(p_ref, _, o_ref):
        for place in range(NEAR_TIMES):
            total = p_ref[place]
            for run in range(1, members // NEAR_TIMES):
                total += p_ref[run * NEAR_TIMES + place]
            for u in range(units):
                at = place * units + u
                row, unit = at // places, at % places
                o_ref[unit // heads, row : row + 1, lanes(unit % heads)] = total[u : u + 1]

    out = jax.ShapeDtypeStruct((kinds, share, heads * lane), F32)
    return small(body, "placed_rows", out, parts, earlier)


def on_device(
    queries,
    grad_out,
    key_value,
    query_logsum,
    query_delta,
    window,
    text_inputs,
    text_grad_out,
    text_logsum,
    text_delta,
    text_length,
):
    t, h = lax.axis_index("tm"), lax.axis_index("height")
    heights = lax.axis_size("height")
    tile, width = queries.shape[2:]

    q = queries.reshape(tile, width)
    g = grad_out.reshape(tile, width)
    kv = key_value.reshape(2 * tile, width)
    info = jnp.stack([t, h, text_length[0], t * heights + h]).astype(jnp.int32)

    piece = text_piece(text_inputs, text_grad_out)
    pack, far = pack_tile(
        info, window.transpose(0, 2, 1), kv, q, g, query_logsum, query_delta, text_logsum
    )
    text = text_whole(piece)
    t1, t2 = swapped(pack, "tm")
    h1, h2 = swapped(joined([pack], t1, t2, piece)[0], "height")

    terms = text_terms(info, pack, text, text_logsum, text_delta, far)
    parts = reduce_times(terms)
    sides = joined([h1, h2], parts)
    corner1, corner2 = swapped(sides, "tm")

    own = summed(parts, sides)
    own = exchange(own.transpose(1, 0, 2), "height")
    near = near_grads(pack, text, text_logsum, text_delta, (h1, h2, t1, t2), far)
    own = summed_heights(own, lax.axis_size("tm"), near)
    own = exchange(own, "tm")
    grad_q, grad_kv, done = far_grads(pack, corner1, corner2, far, near)
    text_grads = placed_rows(own, terms.shape[:3], done)
    return (
        grad_q.reshape(1, 1, tile, width),
        grad_kv.reshape(1, 1, 2, tile, width),
        text_grads,
    )


def solution(mesh):
    placed = (
        P("tm", "height", None, None),
        P("tm", "height", None, None),
        P("tm", "height", None, None, None),
        P("tm", "height", None, None),
        P("tm", "height", None, None),
        P(),
        P(None, "height", None),
        P("height", None),
        P(),
        P(),
        P(),
    )
    return jax.shard_map(
        on_device,
        mesh=mesh,
        in_specs=placed,
        out_specs=(
            P("tm", "height", None, None),
            P("tm", "height", None, None, None),
            P(None, "height", None),
        ),
        check_vma=False,
    )
```
